256 devices in a mesh: cells: 64 (over z, y, core), sub: 4 (over x).
Axes of the slice: x: 4, y: 4, z: 8, core: 2. Of those that a mesh axis runs over, the one named last changes fastest.
Arguments:
- leaf_multipoles: bfloat16 [262144, 296], P(('cells', 'sub')), may hold values from -6 to 6
- occupancy: int32 [262144], P(('cells', 'sub')), may hold values 0 or 1
- upward_maps: bfloat16 [2368, 296], replicated, may hold values from -0.125 to 0.125
- transfer_maps: bfloat16 [9472, 296], replicated, may hold values from -0.125 to 0.125
- downward_maps: bfloat16 [296, 2368], replicated, may hold values from -0.375 to 0.375
- sources_seven: int32 [262144, 8], P(('cells', 'sub')), may hold values from 0 to 262143, as said below
- classes_seven: int32 [262144, 8], P(('cells', 'sub')), may hold values from 0 to 31
- sources_six: int32 [32768, 8], P(('cells', 'sub')), may hold values from 0 to 32767, as said below
- classes_six: int32 [32768, 8], P(('cells', 'sub')), may hold values from 0 to 31
- sources_five: int32 [4096, 8], P(('cells', 'sub')), may hold values from 0 to 4095
- classes_five: int32 [4096, 8], P(('cells', 'sub')), may hold values from 0 to 31
- sources_four: int32 [512, 8], P(('cells', 'sub')), may hold values from 0 to 511
- classes_four: int32 [512, 8], P(('cells', 'sub')), may hold values from 0 to 31
Outputs:
- leaf_locals: bfloat16 [262144, 296], P(('cells', 'sub'))
The draws below stay inside these ranges and needn't reach their ends.
Inputs may be any that keep to these rules, and one draw needn't show every extreme that they name: `sources_seven`: each entry lies within half of 1024 positions of its own cell's index. `sources_six`: each entry lies within half of 128 positions of its own cell's index.
All inputs are finite; a program needn't handle non-finite values. No bound on the sum of `occupancy` on one device may be relied on, other than what follows from the above.
Results may differ from the reference program's by a relative error of at most 0.015.
Values may be sent and summed in bfloat16 or wider, within the bound.
No kernel may reach another device: no remote copies, remote signals or barrier semaphores. Data moves between devices by JAX's collectives and lax.ppermute only.
A program may use at most 128 MiB of HBM per device.

```python
import jax
import jax.numpy as jnp
from jax import lax

COEF = 296
CLASSES = 32
LIST = 8
LEAF_DEV = 1024
L6_DEV = 128
L7_ALL = 262144
L6_ALL = 32768
L5_ALL = 4096
L4_ALL = 512


def near_lists(key, count, reach):
    first_key, second_key = jax.random.split(key)
    target = jnp.arange(count, dtype=jnp.int32)[:, None]
    magnitude = jax.random.randint(first_key, (count, LIST), 1, reach + 1, dtype=jnp.int32)
    direction = jax.random.randint(second_key, (count, LIST), 0, 2, dtype=jnp.int32) * 2 - 1
    return jnp.clip(target + direction * magnitude, 0, count - 1).astype(jnp.int32)


def draw_sources_seven(key, part):
    key = jax.random.fold_in(key, 7)
    return near_lists(key, L7_ALL, LEAF_DEV // 2)


def draw_sources_six(key, part):
    key = jax.random.fold_in(key, 6)
    return near_lists(key, L6_ALL, L6_DEV // 2)


def place_ends(values, key, least, top_value):
    dims = values.shape
    spot = [jax.random.randint(jax.random.fold_in(key, axis), (), 0, dims[axis]) for axis in range(len(dims))]
    values = values.at[tuple(spot)].set(least)
    longest = dims.index(max(dims))
    spot[longest] = (spot[longest] + 1) % dims[longest]
    return values.at[tuple(spot)].set(top_value)


def block_levels(stream_key, extent, shards, low, largest):
    gain = 1.0
    for dim, blocks in shards:
        draws = jax.random.uniform(jax.random.fold_in(jax.random.fold_in(stream_key, 6), dim), (blocks,), jnp.float32, low / len(shards), largest / len(shards))
        gain = gain * jnp.repeat(jnp.exp(draws), extent[dim] // blocks).reshape((-1,) + (1,) * (len(extent) - 1 - dim))
    return gain


def noise(own_key, extent, scale, bound, shards=(), held_as=jnp.bfloat16):
    entries = jax.random.normal(own_key, extent, jnp.float32) * scale
    if len(shards) > 0:
        entries = block_levels(own_key, extent, shards, -0.22, 0.18) * entries
    return jnp.clip(entries, min=-bound, max=bound).astype(held_as)


def setup_inputs(seed: int = 0) -> dict:
    streams_of = jax.random.split(jax.random.key(seed), 14)
    leaf_multipoles = noise(streams_of[0], (L7_ALL, COEF), 1.0, 6.0, ((0, 256),))
    occupancy = place_ends((jax.random.randint(streams_of[1], (L7_ALL,), 0, 4) < 3).astype(jnp.int32), jax.random.fold_in(streams_of[1], 1), 0, 1)
    upward_maps = noise(streams_of[2], (8 * COEF, COEF), (8 * COEF) ** -0.5, 0.125)
    transfer_maps = noise(streams_of[3], (CLASSES * COEF, COEF), (LIST * COEF) ** -0.5, 0.125)
    downward_maps = noise(streams_of[4], (COEF, 8 * COEF), COEF ** -0.5, 0.375)
    sources_seven = draw_sources_seven(jax.random.fold_in(streams_of[13], 71), 0)
    classes_seven = place_ends(jax.random.randint(streams_of[6], (L7_ALL, LIST), 0, CLASSES), jax.random.fold_in(streams_of[6], 1), 0, CLASSES - 1).astype(jnp.int32)
    sources_six = draw_sources_six(jax.random.fold_in(streams_of[13], 71), 0)
    classes_six = place_ends(jax.random.randint(streams_of[8], (L6_ALL, LIST), 0, CLASSES), jax.random.fold_in(streams_of[8], 1), 0, CLASSES - 1).astype(jnp.int32)
    sources_five = place_ends(jax.random.randint(streams_of[9], (L5_ALL, LIST), 0, L5_ALL), jax.random.fold_in(streams_of[9], 1), 0, L5_ALL - 1).astype(jnp.int32)
    classes_five = place_ends(jax.random.randint(streams_of[10], (L5_ALL, LIST), 0, CLASSES), jax.random.fold_in(streams_of[10], 1), 0, CLASSES - 1).astype(jnp.int32)
    sources_four = place_ends(jax.random.randint(streams_of[11], (L4_ALL, LIST), 0, L4_ALL), jax.random.fold_in(streams_of[11], 1), 0, L4_ALL - 1).astype(jnp.int32)
    classes_four = place_ends(jax.random.randint(streams_of[12], (L4_ALL, LIST), 0, CLASSES), jax.random.fold_in(streams_of[12], 1), 0, CLASSES - 1).astype(jnp.int32)
    return dict(leaf_multipoles=leaf_multipoles, occupancy=occupancy, upward_maps=upward_maps, transfer_maps=transfer_maps, downward_maps=downward_maps, sources_seven=sources_seven, classes_seven=classes_seven, sources_six=sources_six, classes_six=classes_six, sources_five=sources_five, classes_five=classes_five, sources_four=sources_four, classes_four=classes_four)


def ascend(children, upward_maps):
    width = children.shape[1]
    merged = children.reshape(-1, 8 * width)
    return jnp.dot(merged, upward_maps, preferred_element_type=jnp.float32).astype(jnp.bfloat16)


def descend(parents, downward_maps):
    width = parents.shape[1]
    spread = jnp.dot(parents, downward_maps, preferred_element_type=jnp.float32)
    return spread.reshape(-1, width)


def far_field(multi, sources, classes, transfer_maps):
    count = sources.shape[0]
    width = multi.shape[1]
    kinds = transfer_maps.shape[0] // width
    blocked = min(count, 512)

    def one_block(pair):
        src_rows, class_rows = pair
        picked = jnp.take(multi, src_rows, axis=0).astype(jnp.float32)
        onehot = (class_rows[:, :, None] == jnp.arange(kinds, dtype=jnp.int32)[None, None, :]).astype(jnp.float32)
        grouped = jnp.einsum('tjc,tjk->tck', onehot, picked, preferred_element_type=jnp.float32)
        grouped = grouped.astype(jnp.bfloat16).reshape(blocked, kinds * width)
        return jnp.dot(grouped, transfer_maps, preferred_element_type=jnp.float32)

    result = lax.map(one_block, (sources.reshape(-1, blocked, sources.shape[1]), classes.reshape(-1, blocked, classes.shape[1])))
    return result.reshape(count, width)


def reference(leaf_multipoles, occupancy, upward_maps, transfer_maps, downward_maps, sources_seven, classes_seven, sources_six, classes_six, sources_five, classes_five, sources_four, classes_four):
    multi_seven = jnp.where(occupancy[:, None] > 0, leaf_multipoles, jnp.zeros_like(leaf_multipoles))
    multi_six = ascend(multi_seven, upward_maps)
    multi_five = ascend(multi_six, upward_maps)
    multi_four = ascend(multi_five, upward_maps)
    local_four = far_field(multi_four, sources_four, classes_four, transfer_maps).astype(jnp.bfloat16)
    local_five = (descend(local_four, downward_maps) + far_field(multi_five, sources_five, classes_five, transfer_maps)).astype(jnp.bfloat16)
    local_six = (descend(local_five, downward_maps) + far_field(multi_six, sources_six, classes_six, transfer_maps)).astype(jnp.bfloat16)
    local_seven = (descend(local_six, downward_maps) + far_field(multi_seven, sources_seven, classes_seven, transfer_maps)).astype(jnp.bfloat16)
    return local_seven
```

```python
import functools

import jax
import jax.numpy as jnp
from jax import lax
from jax.experimental import pallas as pl
from jax.experimental.pallas import tpu as pltpu
from jax.sharding import PartitionSpec as P

F = 296
KINDS = 32
LIST = 8
BF = jnp.bfloat16
F32 = jnp.float32
VM = pl.BlockSpec(memory_space=pltpu.VMEM)
ANY = pl.BlockSpec(memory_space=pl.ANY)
SM = pl.BlockSpec(memory_space=pltpu.SMEM)


def dot(a, b):
    return jnp.dot(a, b, preferred_element_type=F32)


def onehot(rel, depth):
    count = rel.shape[1]
    rows = lax.broadcasted_iota(jnp.int32, (depth, count), 0)
    return jnp.where(rows == rel, 1.0, 0.0).astype(BF)


def split_octants(children, first, width):
    count = children.shape[1]
    source = lax.broadcasted_iota(jnp.int32, (count, 2 * width), 0)
    place = lax.broadcasted_iota(jnp.int32, (count, 2 * width), 1)
    second = (place >= width).astype(jnp.int32)
    wanted = 8 * (place - width * second) + first + second
    return dot(children, jnp.where(source == wanted, 1.0, 0.0).astype(BF))


def ascend(children, up_ref, stack):
    for pair in range(4):
        both = split_octants(children, 2 * pair, 128)
        stack[2 * pair * F : (2 * pair + 1) * F, :] = both[:, :128]
        stack[(2 * pair + 1) * F : (2 * pair + 2) * F, :] = both[:, 128:]
    return dot(up_ref[...], stack[...].astype(BF))


def rise_body(lo_ref, hi_ref, up_ref, six_ref, five_ref, stack):
    children = jnp.concatenate([lo_ref[...], hi_ref[...]], axis=1)
    six = ascend(children, up_ref, stack).astype(BF)
    six_ref[...] = six
    five = ascend(six, up_ref, stack)
    five_ref[...] = five.T[:16, :].astype(BF)


def rise(lo, hi, up):
    return pl.pallas_call(
        rise_body,
        out_shape=(
            jax.ShapeDtypeStruct((F, 128), BF),
            jax.ShapeDtypeStruct((16, F), BF),
        ),
        in_specs=[VM] * 3,
        out_specs=(VM, VM),
        scratch_shapes=[pltpu.VMEM((8 * F, 128), F32)],
        compiler_params=pltpu.CompilerParams(vmem_limit_bytes=24 * 2**20),
        cost_estimate=pl.CostEstimate(flops=2 * 10**9, bytes_accessed=3 * 10**6, transcendentals=0),
        name="rise",
    )(lo, hi, up)


def spread(value, even, odd, slot, lanes):
    blank = jnp.zeros((8, value.shape[1]), F32)
    even[slot, :, lanes] = jnp.concatenate([value, blank], axis=0).astype(BF)
    odd[slot, :, lanes] = jnp.concatenate([blank, value], axis=0).astype(BF)


def stack_pair(grouped, row, lanes, even_tile, odd_tile):
    for i in range(18):
        grouped[pl.ds(row + 16 * i, 16), lanes] = even_tile(i)
    grouped[pl.ds(row + 288, 16), lanes] = even_tile(18) + odd_tile(0)
    for i in range(1, 19):
        grouped[pl.ds(row + 288 + 16 * i, 16), lanes] = odd_tile(i)


def group(labels, even, odd, grouped):
    count = grouped.shape[1]
    wide = [jnp.broadcast_to(label, (16, count)) for label in labels]

    def masks(kind):
        return [jnp.where(label == kind, 1.0, 0.0).astype(BF) for label in wide]

    def total(ref, mask, i):
        terms = [ref[j, 16 * i : 16 * i + 16, :] * mask[j] for j in range(LIST)]
        while len(terms) > 1:
            terms = [terms[q] + terms[q + 1] for q in range(0, len(terms), 2)]
        return terms[0]

    def pair(p, carry):
        first, second = masks(2 * p), masks(2 * p + 1)
        stack_pair(
            grouped,
            pl.multiple_of(p * 2 * F, 16),
            slice(None),
            lambda i: total(even, first, i),
            lambda i: total(odd, second, i),
        )
        return carry

    lax.fori_loop(0, KINDS // 2, pair, 0)


def transfer(maps, grouped, out_ref):
    out_ref[...] = dot(maps[:, :256], grouped[:256, :])

    def part(i, carry):
        at = pl.multiple_of(256 + i * 2304, 256)
        out_ref[...] += dot(maps[:, pl.ds(at, 2304)], grouped[pl.ds(at, 2304), :])
        return carry

    lax.fori_loop(0, 4, part, 0)


def near_body(block, a_ref, b_ref, c_ref, src_ref, cls_ref, maps_hbm, out_ref, maps, even, odd, grouped, sem):
    copy = pltpu.make_async_copy(maps_hbm, maps, sem)
    copy.start()
    lanes = slice(256 * block, 256 * block + 256)
    first = (a_ref, b_ref, c_ref)
    base = 256 * block if block < 2 else 256 * block - 512
    window = jnp.concatenate([ref[...] for ref in first], axis=1)[:, base : base + 1280]

    def one(j, carry):
        rel = src_ref[pl.ds(j, 1), lanes] - 256 * block
        spread(dot(window, onehot(rel, 1280)), even, odd, j, slice(None))
        return carry

    lax.fori_loop(0, LIST, one, 0)
    group([cls_ref[j : j + 1, lanes] for j in range(LIST)], even, odd, grouped)
    copy.wait()
    transfer(maps, grouped, out_ref)


def far_scratch(count):
    return [
        pltpu.VMEM((F, KINDS * F), BF),
        pltpu.VMEM((LIST, F + 8, count), BF),
        pltpu.VMEM((LIST, F + 8, count), BF),
        pltpu.VMEM((KINDS * F, count), BF),
        pltpu.SemaphoreType.DMA,
    ]


def near(block, a, b, c, src, cls, maps):
    return pl.pallas_call(
        functools.partial(near_body, block),
        out_shape=jax.ShapeDtypeStruct((F, 256), F32),
        in_specs=[VM] * 5 + [ANY],
        out_specs=VM,
        scratch_shapes=far_scratch(256),
        compiler_params=pltpu.CompilerParams(vmem_limit_bytes=28 * 2**20),
        cost_estimate=pl.CostEstimate(flops=6 * 10**9, bytes_accessed=6 * 10**6, transcendentals=0),
        name=f"near{block}",
    )(a, b, c, src, cls, maps)


def middle_body(below_ref, above_ref, six_ref, up_ref, src_ref, cls_ref, maps_hbm, out_ref, maps, even, odd, grouped, sem, stack):
    copy = pltpu.make_async_copy(maps_hbm, maps, sem)
    copy.start()
    children = jnp.concatenate([below_ref[...], above_ref[...]], axis=1)
    halo = ascend(children, up_ref, stack).astype(BF)
    window = jnp.concatenate([six_ref[...], halo], axis=1)

    def one(j, carry):
        rel = src_ref[pl.ds(j, 1), :]
        spread(dot(window, onehot(rel, 256)), even, odd, j, slice(None))
        return carry

    lax.fori_loop(0, LIST, one, 0)
    group([cls_ref[j : j + 1, :] for j in range(LIST)], even, odd, grouped)
    copy.wait()
    transfer(maps, grouped, out_ref)


def middle(below, above, six, up, src, cls, maps):
    return pl.pallas_call(
        middle_body,
        out_shape=jax.ShapeDtypeStruct((F, 128), F32),
        in_specs=[VM] * 6 + [ANY],
        out_specs=VM,
        scratch_shapes=far_scratch(128) + [pltpu.VMEM((8 * F, 128), F32)],
        compiler_params=pltpu.CompilerParams(vmem_limit_bytes=28 * 2**20),
        cost_estimate=pl.CostEstimate(flops=4 * 10**9, bytes_accessed=6 * 10**6, transcendentals=0),
        name="middle",
    )(below, above, six, up, src, cls, maps)


def descend(parents, down_ref, even, odd, stack, count):
    wide = min(count, 256)

    def chunk(q, carry):
        parent = lax.broadcasted_iota(jnp.int32, (128, wide), 0)
        child = lax.broadcasted_iota(jnp.int32, (128, wide), 1) + q * wide
        copies = dot(parents, jnp.where(child // 8 == parent, 1.0, 0.0).astype(BF))
        spread(copies, even, odd, 0, slice(0, wide))
        octant = lax.broadcasted_iota(jnp.int32, (16, wide), 1) % 8
        lanes = pl.ds(pl.multiple_of(q * wide, wide), wide)
        for p in range(4):
            first = jnp.where(octant == 2 * p, 1.0, 0.0).astype(BF)
            second = jnp.where(octant == 2 * p + 1, 1.0, 0.0).astype(BF)
            stack_pair(
                stack,
                p * 2 * F,
                lanes,
                lambda i: even[0, 16 * i : 16 * i + 16, :wide] * first,
                lambda i: odd[0, 16 * i : 16 * i + 16, :wide] * second,
            )
        return carry

    if count == wide:
        chunk(0, 0)
    else:
        lax.fori_loop(0, count // wide, chunk, 0)


def last_body(
    t0, t1, t2, t3, t4, t5, t6, t7, index_ref, cls_ref, up_ref, down_ref, six_ref,
    s0, s1, s2, s3, maps_hbm, out_ref,
    maps, even, odd, grouped, sem, rise_stack, coarse, fall_stack, wide_even, wide_odd,
):
    copy = pltpu.make_async_copy(maps_hbm, maps, sem)
    copy.start()
    wanted = index_ref[...]
    picked = jnp.zeros((F, 256), F32)
    for k, table in enumerate((t0, t1, t2, t3, t4, t5, t6, t7)):
        picked += dot(table[...], onehot(wanted - 512 * k, 512))
    even[...] = jnp.zeros(even.shape, BF)
    odd[...] = jnp.zeros(odd.shape, BF)
    rise_stack[...] = jnp.zeros(rise_stack.shape, F32)
    for o in range(8):
        rise_stack[o * F : (o + 1) * F, :16] = picked[:, 128 + 16 * o : 144 + 16 * o]
    four = dot(up_ref[...], rise_stack[...].astype(BF)).astype(BF).astype(F32)
    blank = jnp.zeros((F, 110), F32)
    for j in range(LIST):
        both = jnp.concatenate([picked[:, 16 * j : 16 * j + 16], four[:, 2 * j : 2 * j + 2], blank], axis=1)
        spread(both, even, odd, j, slice(None))
    group([cls_ref[j : j + 1, :] for j in range(LIST)], even, odd, grouped)
    copy.wait()
    transfer(maps, grouped, coarse)
    lane = lax.broadcasted_iota(jnp.int32, (F, 128), 1)
    far_five = jnp.where(lane < 16, coarse[...], 0.0)
    take = lax.broadcasted_iota(jnp.int32, (128, 128), 0) == lax.broadcasted_iota(jnp.int32, (128, 128), 1) + 16
    local = dot(coarse[...].astype(BF), jnp.where(take, 1.0, 0.0).astype(BF)).astype(BF)
    descend(local, down_ref, wide_even, wide_odd, fall_stack, 128)
    local = (dot(down_ref[...], fall_stack[:, :128]) + far_five).astype(BF)
    descend(local, down_ref, wide_even, wide_odd, fall_stack, 128)
    local = (dot(down_ref[...], fall_stack[:, :128]) + six_ref[...]).astype(BF)
    descend(local, down_ref, wide_even, wide_odd, fall_stack, 1024)
    for q, seven in enumerate((s0, s1, s2, s3)):
        lanes = slice(256 * q, 256 * q + 256)
        out_ref[:, lanes] = (dot(down_ref[...], fall_stack[:, lanes]) + seven[...]).astype(BF)


def last(tables, index, cls, up, down, six, sevens, maps):
    return pl.pallas_call(
        last_body,
        out_shape=jax.ShapeDtypeStruct((F, 1024), BF),
        in_specs=[VM] * 17 + [ANY],
        out_specs=VM,
        scratch_shapes=far_scratch(128)
        + [
            pltpu.VMEM((8 * F, 128), F32),
            pltpu.VMEM((F, 128), F32),
            pltpu.VMEM((8 * F, 1024), BF),
            pltpu.VMEM((1, F + 8, 256), BF),
            pltpu.VMEM((1, F + 8, 256), BF),
        ],
        compiler_params=pltpu.CompilerParams(vmem_limit_bytes=40 * 2**20),
        cost_estimate=pl.CostEstimate(flops=8 * 10**9, bytes_accessed=12 * 10**6, transcendentals=0),
        name="last",
    )(*tables, index, cls, up, down, six, *sevens, maps)


def shifted(value, axis, steps):
    count = lax.axis_size(axis)
    first, last_one = (max(0, -steps), min(count, count - steps))
    return lax.ppermute(value, axis, [(source, source + steps) for source in range(first, last_one)])


def turned(value, axis, size, stride, steps):
    pairs = []
    for source in range(lax.axis_size(axis)):
        position = (source // stride) % size
        target = source + ((position + steps) % size - position) * stride
        pairs.append((source, target))
    return lax.ppermute(value, axis, pairs)


along_z = lambda value, steps: turned(value, "cells", 8, 8, steps)
along_y = lambda value, steps: turned(value, "cells", 4, 2, steps)
along_core = lambda value, steps: turned(value, "cells", 2, 1, steps)
along_x = lambda value, steps: turned(value, "sub", 4, 1, steps)


def body(
    leaf_multipoles,
    occupancy,
    upward_maps,
    transfer_maps,
    downward_maps,
    sources_seven,
    classes_seven,
    sources_six,
    classes_six,
    sources_five,
    classes_five,
    sources_four,
    classes_four,
):
    leaves = leaf_multipoles.T
    up, maps = upward_maps.T, transfer_maps.T
    down = downward_maps.reshape(F, 8, F).transpose(2, 1, 0).reshape(F, 8 * F)
    masked = jnp.where(occupancy[None, :] > 0, leaves, jnp.zeros_like(leaves))
    lo, hi = masked[:, :512], masked[:, 512:]
    below = shifted(hi, ("cells", "sub"), 1)
    above = shifted(lo, ("cells", "sub"), -1)
    six, five = rise(lo, hi, up)

    cells, sub = lax.axis_index("cells"), lax.axis_index("sub")
    place = cells * 4 + sub
    src_seven = sources_seven.T - (place * 1024 - 512)
    cls_seven = classes_seven.T
    rel_six = sources_six.T - (place * 128 - 64)
    src_six = jnp.where(rel_six < 64, rel_six + 128, jnp.where(rel_six < 192, rel_six - 64, rel_six))

    minus, plus = along_z(five, 1), along_z(five, -1)
    three = jnp.stack([minus, five, plus])
    upper = along_z(three, -3)
    lower = along_z(three[1:], 3)
    column = jnp.concatenate([lower, three, upper], axis=0).reshape(128, F).T
    plane = jnp.concatenate([column, along_y(column, -1), along_y(column, 2), along_y(column, 1)], axis=1)
    tables = [plane, along_x(plane, -1), along_x(plane, 2), along_x(plane, 1)]
    tables = tables + [along_core(table, 1) for table in tables]

    def where_held(cell):
        device = cell // 16
        there = (device // 4, device % 4)
        dz = (there[0] // 8 - cells // 8 + 3) % 8
        dy = (there[0] // 2 - cells // 2) % 4
        dc = (there[0] - cells) % 2
        dx = (there[1] - sub) % 4
        return (dc * 4 + dx) * 512 + dy * 128 + dz * 16 + cell % 16

    entries_five = sources_five.T.reshape(1, 128)
    entries_four = sources_four.T.reshape(1, 16)
    octants = jnp.arange(8, dtype=jnp.int32)[:, None]
    children = (8 * entries_four + octants).reshape(1, 128)
    index = where_held(jnp.concatenate([entries_five, children], axis=1))
    cls_coarse = jnp.concatenate(
        [classes_five.T, classes_four.T, jnp.full((LIST, 110), KINDS, jnp.int32)], axis=1
    )

    sevens = [
        near(0, below, lo, hi, src_seven, cls_seven, maps),
        near(1, below, lo, hi, src_seven, cls_seven, maps),
        near(2, lo, hi, above, src_seven, cls_seven, maps),
        near(3, lo, hi, above, src_seven, cls_seven, maps),
    ]
    far_six = middle(below, above, six, up, src_six, classes_six.T, maps)
    return last(tables, index, cls_coarse, up, down, far_six, sevens, maps).T


def solution(mesh):
    in_specs = (
        P(("cells", "sub"), None),
        P(("cells", "sub")),
        P(),
        P(),
        P(),
        P(("cells", "sub"), None),
        P(("cells", "sub"), None),
        P(("cells", "sub"), None),
        P(("cells", "sub"), None),
        P(("cells", "sub"), None),
        P(("cells", "sub"), None),
        P(("cells", "sub"), None),
        P(("cells", "sub"), None),
    )
    out_specs = P(("cells", "sub"), None)
    return jax.shard_map(body, mesh=mesh, in_specs=in_specs, out_specs=out_specs, check_vma=False)
```

```python
import functools

import jax
import jax.numpy as jnp
from jax import lax
from jax.experimental import pallas as pl
from jax.experimental.pallas import tpu as pltpu
from jax.sharding import PartitionSpec as P

F = 296
KINDS = 32
LIST = 8
BF = jnp.bfloat16
F32 = jnp.float32
VM = pl.BlockSpec(memory_space=pltpu.VMEM)


def dot(a, b):
    return jnp.dot(a, b, preferred_element_type=F32)


def onehot(rel, depth):
    count = rel.shape[1]
    rows = lax.broadcasted_iota(jnp.int32, (depth, count), 0)
    return jnp.where(rows == rel, 1.0, 0.0).astype(BF)


def split_octants(children, first, width):
    count = children.shape[1]
    source = lax.broadcasted_iota(jnp.int32, (count, 2 * width), 0)
    place = lax.broadcasted_iota(jnp.int32, (count, 2 * width), 1)
    second = (place >= width).astype(jnp.int32)
    wanted = 8 * (place - width * second) + first + second
    return dot(children, jnp.where(source == wanted, 1.0, 0.0).astype(BF))


def ascend(children, up_ref, stack):
    for pair in range(4):
        both = split_octants(children, 2 * pair, 128)
        stack[2 * pair * F : (2 * pair + 1) * F, :] = both[:, :128]
        stack[(2 * pair + 1) * F : (2 * pair + 2) * F, :] = both[:, 128:]
    return dot(up_ref[...], stack[...].astype(BF))


def rise_body(leaf_ref, held_ref, up_ref, lo_ref, hi_ref, six_ref, five_ref, stack):
    held = jnp.concatenate([held_ref[r : r + 1, :] for r in range(8)], axis=1)
    children = leaf_ref[...] * jnp.where(held > 0, 1.0, 0.0).astype(BF)
    lo_ref[...] = children[:, :512]
    hi_ref[...] = children[:, 512:]
    six = ascend(children, up_ref, stack).astype(BF)
    six_ref[...] = six
    five = ascend(six, up_ref, stack)
    five_ref[...] = five.T[:16, :].astype(BF)


def rise(leaves, held, up):
    return pl.pallas_call(
        rise_body,
        out_shape=(
            jax.ShapeDtypeStruct((F, 512), BF),
            jax.ShapeDtypeStruct((F, 512), BF),
            jax.ShapeDtypeStruct((F, 128), BF),
            jax.ShapeDtypeStruct((16, F), BF),
        ),
        in_specs=[VM] * 3,
        out_specs=(VM,) * 4,
        scratch_shapes=[pltpu.VMEM((8 * F, 128), F32)],
        compiler_params=pltpu.CompilerParams(vmem_limit_bytes=16 * 2**20),
        cost_estimate=pl.CostEstimate(flops=2 * 10**9, bytes_accessed=3 * 10**6, transcendentals=0),
        name="rise",
    )(leaves, held, up)


def spread(value, even, odd, slot, lanes):
    blank = jnp.zeros((8, value.shape[1]), F32)
    even[slot, :, lanes] = jnp.concatenate([value, blank], axis=0).astype(BF)
    odd[slot, :, lanes] = jnp.concatenate([blank, value], axis=0).astype(BF)


def stack_pair(grouped, row, lanes, even_tile, odd_tile):
    for i in range(18):
        grouped[pl.ds(row + 16 * i, 16), lanes] = even_tile(i)
    grouped[pl.ds(row + 288, 16), lanes] = even_tile(18) + odd_tile(0)
    for i in range(1, 19):
        grouped[pl.ds(row + 288 + 16 * i, 16), lanes] = odd_tile(i)


def group(labels, even, odd, grouped, p):
    wide = [jnp.broadcast_to(label, (16, 256)) for label in labels]

    def masks(kind):
        return [jnp.where(label == kind, 1.0, 0.0).astype(BF) for label in wide]

    first, second = masks(2 * p), masks(2 * p + 1)

    def total(ref, mask, i):
        terms = [ref[j, 16 * i : 16 * i + 16, :] * mask[j] for j in range(LIST)]
        while len(terms) > 1:
            terms = [terms[q] + terms[q + 1] for q in range(0, len(terms), 2)]
        return terms[0]

    stack_pair(
        grouped,
        pl.multiple_of(p * 2 * F, 16),
        slice(None),
        lambda i: total(even, first, i),
        lambda i: total(odd, second, i),
    )


def near_body(block, count, a_ref, b_ref, c_ref, src_ref, cls_ref, maps_ref, out_ref, window, even, odd, grouped):
    side = block % 2
    for k in range(4 + count):
        half = k + side
        window[:, 256 * k : 256 * k + 256] = (a_ref, b_ref, c_ref)[half // 2][:, 256 * (half % 2) : 256 * (half % 2) + 256]

    def pick(i, carry):
        local, four = i // 2, i % 2
        base = pl.multiple_of(local * 256, 256)
        lanes = pl.ds(pl.multiple_of((block + local) * 256, 256), 256)
        start = (block + local) * 256
        wanted = [onehot(src_ref[pl.ds(4 * four + q, 1), lanes] - start, 1280) for q in range(4)]
        value = dot(window[:, pl.ds(base, 1280)], jnp.concatenate(wanted, axis=1))
        for q in range(4):
            spread(value[:, 256 * q : 256 * q + 256], even.at[local], odd.at[local], 4 * four + q, slice(None))
        return carry

    lax.fori_loop(0, 2 * count, pick, 0)

    def sums(i, carry):
        local, p = i // 16, i % 16
        lanes = pl.ds(pl.multiple_of((block + local) * 256, 256), 256)
        labels = [cls_ref[j : j + 1, lanes] for j in range(LIST)]
        group(labels, even.at[local], odd.at[local], grouped.at[local], p)
        return carry

    lax.fori_loop(0, 16 * count, sums, 0)

    def send(i, carry):
        out_ref[i] = dot(maps_ref[...], grouped[i])
        return carry

    lax.fori_loop(0, count, send, 0)


def near(block, count, a, b, c, src, cls, maps):
    return pl.pallas_call(
        functools.partial(near_body, block, count),
        out_shape=jax.ShapeDtypeStruct((count, F, 256), F32),
        in_specs=[VM] * 6,
        out_specs=VM,
        scratch_shapes=[
            pltpu.VMEM((F, 1024 + 256 * count), BF),
            pltpu.VMEM((count, LIST, F + 8, 256), BF),
            pltpu.VMEM((count, LIST, F + 8, 256), BF),
            pltpu.VMEM((count, KINDS * F, 256), BF),
        ],
        compiler_params=pltpu.CompilerParams(vmem_limit_bytes=(22 if count > 1 else 16) * 2**20),
        cost_estimate=pl.CostEstimate(flops=count * 6 * 10**9, bytes_accessed=6 * 10**6, transcendentals=0),
        name=f"near{block}",
    )(a, b, c, src, cls, maps)


def halo_body(below_ref, above_ref, up_ref, out_ref, stack):
    children = jnp.concatenate([below_ref[...], above_ref[...]], axis=1)
    out_ref[...] = ascend(children, up_ref, stack).astype(BF)


def halo_six(below, above, up):
    return pl.pallas_call(
        halo_body,
        out_shape=jax.ShapeDtypeStruct((F, 128), BF),
        in_specs=[VM] * 3,
        out_specs=VM,
        scratch_shapes=[pltpu.VMEM((8 * F, 128), F32)],
        compiler_params=pltpu.CompilerParams(vmem_limit_bytes=16 * 2**20),
        cost_estimate=pl.CostEstimate(flops=2 * 10**9, bytes_accessed=3 * 10**6, transcendentals=0),
        name="halo",
    )(below, above, up)


def flip_body(down_ref, out_ref):
    out_ref[...] = down_ref[...].T


def flip(down):
    return pl.pallas_call(
        flip_body,
        out_shape=jax.ShapeDtypeStruct((8 * F, F), BF),
        in_specs=[VM],
        out_specs=VM,
        compiler_params=pltpu.CompilerParams(vmem_limit_bytes=16 * 2**20),
        cost_estimate=pl.CostEstimate(flops=10**9, bytes_accessed=3 * 10**6, transcendentals=0),
        name="flip",
    )(down)


def last_body(
    t0, t1, t2, t3, t4, t5, t6, t7, index_ref, six_ref, halo_ref, src_ref, cls_ref, up_ref, down_ref,
    s0, s1, s2, maps_ref, out_ref,
    even, odd, grouped, stack, coarse, both, weave, fars, local,
):
    window = jnp.concatenate([six_ref[...], halo_ref[...]], axis=1)

    def pick(i, carry):
        wanted = jnp.concatenate([src_ref[pl.ds(2 * i, 1), :], src_ref[pl.ds(2 * i + 1, 1), :]], axis=1)
        value = dot(window, onehot(wanted, 256))
        for q in range(2):
            spread(value[:, 128 * q : 128 * q + 128], even, odd, 2 * i + q, slice(128, 256))
        return carry

    lax.fori_loop(0, LIST // 2, pick, 0)

    wanted = index_ref[...]
    picked = jnp.zeros((F, 256), F32)
    for k, table in enumerate((t0, t1, t2, t3, t4, t5, t6, t7)):
        picked += dot(table[...], onehot(wanted - 512 * k, 512))
    stack[...] = jnp.zeros(stack.shape, F32)
    for o in range(8):
        stack[o * F : (o + 1) * F, :16] = picked[:, 128 + 16 * o : 144 + 16 * o]
    four = dot(up_ref[...], stack[...].astype(BF)).astype(BF).astype(F32)
    blank = jnp.zeros((F, 110), F32)
    for j in range(LIST):
        value = jnp.concatenate([picked[:, 16 * j : 16 * j + 16], four[:, 2 * j : 2 * j + 2], blank], axis=1)
        spread(value, even, odd, j, slice(0, 128))

    def sums(p, carry):
        group([cls_ref[j : j + 1, :] for j in range(LIST)], even, odd, grouped, p)
        return carry

    lax.fori_loop(0, KINDS // 2, sums, 0)
    coarse[...] = dot(maps_ref[...], grouped[...])

    def fill(o, carry):
        row = lax.broadcasted_iota(jnp.int32, (128, 1024), 0)
        cell = lax.broadcasted_iota(jnp.int32, (128, 1024), 1)
        weave[pl.ds(pl.multiple_of(o * 128, 128), 128), :] = jnp.where(cell == 8 * row + o, 1.0, 0.0).astype(BF)
        return carry

    lax.fori_loop(0, 8, fill, 0)
    both[...] = jnp.zeros(both.shape, BF)
    lane = lax.broadcasted_iota(jnp.int32, (F, 128), 1)
    fars[0] = jnp.where(lane < 16, coarse[:, :128], 0.0)
    fars[1] = coarse[:, 128:]
    take = lax.broadcasted_iota(jnp.int32, (128, 128), 0) == lax.broadcasted_iota(jnp.int32, (128, 128), 1) + 16
    local[...] = dot(coarse[:, :128].astype(BF), jnp.where(take, 1.0, 0.0).astype(BF)).astype(BF)

    def woven(lanes):
        pieces = dot(both[...], weave[:, lanes])
        return pieces[:F, :] + pieces[304 : 304 + F, :]

    def fall(level, carry):
        children = dot(down_ref[...], local[...])
        for o in range(8):
            part = children[o * F : (o + 1) * F, :]
            high = part.astype(BF)
            both[:F, 128 * o : 128 * o + 128] = high
            both[304 : 304 + F, 128 * o : 128 * o + 128] = (part - high.astype(F32)).astype(BF)

        @pl.when(level < 2)
        def _():
            local[...] = (woven(slice(0, 128)) + fars[jnp.minimum(level, 1)]).astype(BF)

        return carry

    lax.fori_loop(0, 3, fall, 0)
    for q, seven in enumerate((s0.at[0], s1.at[0], s2.at[0], s2.at[1])):
        lanes = slice(256 * q, 256 * q + 256)
        out_ref[:, lanes] = (woven(lanes) + seven[...]).astype(BF)


def last(tables, index, six, halo, src, cls, up, down, sevens, maps):
    return pl.pallas_call(
        last_body,
        out_shape=jax.ShapeDtypeStruct((F, 1024), BF),
        in_specs=[VM] * 19,
        out_specs=VM,
        scratch_shapes=[
            pltpu.VMEM((LIST, F + 8, 256), BF),
            pltpu.VMEM((LIST, F + 8, 256), BF),
            pltpu.VMEM((KINDS * F, 256), BF),
            pltpu.VMEM((8 * F, 128), F32),
            pltpu.VMEM((F, 256), F32),
            pltpu.VMEM((608, 1024), BF),
            pltpu.VMEM((1024, 1024), BF),
            pltpu.VMEM((2, F, 128), F32),
            pltpu.VMEM((F, 128), BF),
        ],
        compiler_params=pltpu.CompilerParams(vmem_limit_bytes=24 * 2**20),
        cost_estimate=pl.CostEstimate(flops=8 * 10**9, bytes_accessed=12 * 10**6, transcendentals=0),
        name="last",
    )(*tables, index, six, halo, src, cls, up, down, *sevens, maps)


def shifted(value, axis, steps):
    count = lax.axis_size(axis)
    first, last_one = (max(0, -steps), min(count, count - steps))
    return lax.ppermute(value, axis, [(source, source + steps) for source in range(first, last_one)])


def turned(value, axis, size, stride, steps):
    pairs = []
    for source in range(lax.axis_size(axis)):
        position = (source // stride) % size
        target = source + ((position + steps) % size - position) * stride
        pairs.append((source, target))
    return lax.ppermute(value, axis, pairs)


along_z = lambda value, steps: turned(value, "cells", 8, 8, steps)
along_y = lambda value, steps: turned(value, "cells", 4, 2, steps)
along_core = lambda value, steps: turned(value, "cells", 2, 1, steps)
along_x = lambda value, steps: turned(value, "sub", 4, 1, steps)


def tie(*values):
    return lax.optimization_barrier(values)


def body(
    leaf_multipoles,
    occupancy,
    upward_maps,
    transfer_maps,
    downward_maps,
    sources_seven,
    classes_seven,
    sources_six,
    classes_six,
    sources_five,
    classes_five,
    sources_four,
    classes_four,
):
    leaves = leaf_multipoles.T
    up, maps = upward_maps.T, transfer_maps.T
    lo, hi, six, five = rise(leaves, occupancy.reshape(8, 128), up)
    below = shifted(hi, ("cells", "sub"), 1)
    above = shifted(lo, ("cells", "sub"), -1)

    cells, sub = lax.axis_index("cells"), lax.axis_index("sub")
    place = cells * 4 + sub
    src_seven = sources_seven.T - (place * 1024 - 512)
    cls_seven = classes_seven.T
    rel_six = sources_six.T - (place * 128 - 64)
    src_six = jnp.where(rel_six < 64, rel_six + 128, jnp.where(rel_six < 192, rel_six - 64, rel_six))

    down = flip(downward_maps)
    minus, plus = along_z(five, 1), along_z(five, -1)
    three = jnp.stack([minus, five, plus])
    three, near_lo = tie(three, lo)
    upper = along_z(three, -3)
    lower = along_z(three[1:], 3)
    seven_0 = near(0, 1, below, near_lo, hi, src_seven, cls_seven, maps)
    column = jnp.concatenate([lower, three, upper], axis=0).reshape(128, F).T
    column, seven_0, near_lo = tie(column, seven_0, near_lo)
    sides = along_y(column, -1), along_y(column, 2), along_y(column, 1)
    seven_1 = near(1, 1, below, near_lo, hi, src_seven, cls_seven, maps)
    plane = jnp.concatenate([column, *sides], axis=1)
    plane, seven_1, near_lo, near_up = tie(plane, seven_1, near_lo, up)
    tables = [plane, along_x(plane, -1), along_x(plane, 2), along_x(plane, 1)]
    halo = halo_six(below, above, near_up)
    seven_2 = near(2, 2, near_lo, hi, above, src_seven, cls_seven, maps)
    *tables, seven_2, halo = tie(*tables, seven_2, halo)
    tables = tables + [along_core(table, 1) for table in tables]
    sevens = [seven_0, seven_1, seven_2]

    def where_held(cell):
        device = cell // 16
        there = (device // 4, device % 4)
        dz = (there[0] // 8 - cells // 8 + 3) % 8
        dy = (there[0] // 2 - cells // 2) % 4
        dc = (there[0] - cells) % 2
        dx = (there[1] - sub) % 4
        return (dc * 4 + dx) * 512 + dy * 128 + dz * 16 + cell % 16

    entries_five = sources_five.T.reshape(1, 128)
    entries_four = sources_four.T.reshape(1, 16)
    octants = jnp.arange(8, dtype=jnp.int32)[:, None]
    children = (8 * entries_four + octants).reshape(1, 128)
    index = where_held(jnp.concatenate([entries_five, children], axis=1))
    cls_low = jnp.concatenate(
        [classes_five.T, classes_four.T, jnp.full((LIST, 110), KINDS, jnp.int32), classes_six.T], axis=1
    )
    return last(tables, index, six, halo, src_six, cls_low, up, down, sevens, maps).T


def solution(mesh):
    in_specs = (
        P(("cells", "sub"), None),
        P(("cells", "sub")),
        P(),
        P(),
        P(),
        P(("cells", "sub"), None),
        P(("cells", "sub"), None),
        P(("cells", "sub"), None),
        P(("cells", "sub"), None),
        P(("cells", "sub"), None),
        P(("cells", "sub"), None),
        P(("cells", "sub"), None),
        P(("cells", "sub"), None),
    )
    out_specs = P(("cells", "sub"), None)
    return jax.shard_map(body, mesh=mesh, in_specs=in_specs, out_specs=out_specs, check_vma=False)
```

```python
import functools

import jax
import jax.numpy as jnp
from jax import lax
from jax.experimental import pallas as pl
from jax.experimental.pallas import tpu as pltpu
from jax.sharding import PartitionSpec as P

F = 296
KINDS = 32
LIST = 8
BF = jnp.bfloat16
F32 = jnp.float32
VM = pl.BlockSpec(memory_space=pltpu.VMEM)


def dot(a, b):
    return jnp.dot(a, b, preferred_element_type=F32)


def onehot(rel, depth):
    count = rel.shape[1]
    rows = lax.broadcasted_iota(jnp.int32, (depth, count), 0)
    return jnp.where(rows == rel, 1.0, 0.0).astype(BF)


def split_octants(children, first, width):
    count = children.shape[1]
    source = lax.broadcasted_iota(jnp.int32, (count, 2 * width), 0)
    place = lax.broadcasted_iota(jnp.int32, (count, 2 * width), 1)
    second = (place >= width).astype(jnp.int32)
    wanted = 8 * (place - width * second) + first + second
    return dot(children, jnp.where(source == wanted, 1.0, 0.0).astype(BF))


def ascend(children, up_ref, stack):
    for pair in range(4):
        both = split_octants(children, 2 * pair, 128)
        stack[2 * pair * F : (2 * pair + 1) * F, :] = both[:, :128]
        stack[(2 * pair + 1) * F : (2 * pair + 2) * F, :] = both[:, 128:]
    return dot(up_ref[...], stack[...].astype(BF))


def rise_body(lo_ref, hi_ref, up_ref, six_ref, five_ref, stack):
    children = jnp.concatenate([lo_ref[...], hi_ref[...]], axis=1)
    six = ascend(children, up_ref, stack).astype(BF)
    six_ref[...] = six
    five = ascend(six, up_ref, stack)
    five_ref[...] = five.T[:16, :].astype(BF)


def rise(lo, hi, up):
    return pl.pallas_call(
        rise_body,
        out_shape=(
            jax.ShapeDtypeStruct((F, 128), BF),
            jax.ShapeDtypeStruct((16, F), BF),
        ),
        in_specs=[VM] * 3,
        out_specs=(VM,) * 2,
        scratch_shapes=[pltpu.VMEM((8 * F, 128), F32)],
        compiler_params=pltpu.CompilerParams(vmem_limit_bytes=16 * 2**20),
        cost_estimate=pl.CostEstimate(flops=8 * 10**9, bytes_accessed=3 * 10**6, transcendentals=0),
        name="rise",
    )(lo, hi, up)


def spread(value, even, odd, slot, lanes):
    blank = jnp.zeros((8, value.shape[1]), F32)
    even[slot, :, lanes] = jnp.concatenate([value, blank], axis=0).astype(BF)
    odd[slot, :, lanes] = jnp.concatenate([blank, value], axis=0).astype(BF)


def stack_pair(grouped, row, lanes, even_tile, odd_tile):
    for i in range(18):
        grouped[pl.ds(row + 16 * i, 16), lanes] = even_tile(i)
    grouped[pl.ds(row + 288, 16), lanes] = even_tile(18) + odd_tile(0)
    for i in range(1, 19):
        grouped[pl.ds(row + 288 + 16 * i, 16), lanes] = odd_tile(i)


def group(labels, even, odd, grouped, p):
    wide = [jnp.broadcast_to(label, (16, 256)) for label in labels]

    def masks(kind):
        return [jnp.where(label == kind, 1.0, 0.0).astype(BF) for label in wide]

    first, second = masks(2 * p), masks(2 * p + 1)

    def total(ref, mask, i):
        terms = [ref[j, 16 * i : 16 * i + 16, :] * mask[j] for j in range(LIST)]
        while len(terms) > 1:
            terms = [terms[q] + terms[q + 1] for q in range(0, len(terms), 2)]
        return terms[0]

    stack_pair(
        grouped,
        pl.multiple_of(p * 2 * F, 16),
        slice(None),
        lambda i: total(even, first, i),
        lambda i: total(odd, second, i),
    )


def near_body(block, count, a_ref, b_ref, c_ref, src_ref, cls_ref, maps_ref, out_ref, window, even, odd, grouped):
    side = block % 2
    for k in range(4 + count):
        half = k + side
        window[:, 256 * k : 256 * k + 256] = (a_ref, b_ref, c_ref)[half // 2][:, 256 * (half % 2) : 256 * (half % 2) + 256]

    def pick(i, carry):
        local, four = i // 2, i % 2
        base = pl.multiple_of(local * 256, 256)
        lanes = pl.ds(pl.multiple_of((block + local) * 256, 256), 256)
        start = (block + local) * 256
        wanted = [onehot(src_ref[pl.ds(4 * four + q, 1), lanes] - start, 1280) for q in range(4)]
        value = dot(window[:, pl.ds(base, 1280)], jnp.concatenate(wanted, axis=1))
        for q in range(4):
            spread(value[:, 256 * q : 256 * q + 256], even.at[local], odd.at[local], 4 * four + q, slice(None))
        return carry

    lax.fori_loop(0, 2 * count, pick, 0)

    def sums(i, carry):
        local, p = i // 16, i % 16
        lanes = pl.ds(pl.multiple_of((block + local) * 256, 256), 256)
        labels = [cls_ref[j : j + 1, lanes] for j in range(LIST)]
        group(labels, even.at[local], odd.at[local], grouped.at[local], p)
        return carry

    lax.fori_loop(0, 16 * count, sums, 0)

    def send(i, carry):
        out_ref[i] = dot(maps_ref[...], grouped[i])
        return carry

    lax.fori_loop(0, count, send, 0)


def near(block, count, a, b, c, src, cls, maps):
    return pl.pallas_call(
        functools.partial(near_body, block, count),
        out_shape=jax.ShapeDtypeStruct((count, F, 256), F32),
        in_specs=[VM] * 6,
        out_specs=VM,
        scratch_shapes=[
            pltpu.VMEM((F, 1024 + 256 * count), BF),
            pltpu.VMEM((count, LIST, F + 8, 256), BF),
            pltpu.VMEM((count, LIST, F + 8, 256), BF),
            pltpu.VMEM((count, KINDS * F, 256), BF),
        ],
        compiler_params=pltpu.CompilerParams(vmem_limit_bytes=(22 if count > 1 else 16) * 2**20),
        cost_estimate=pl.CostEstimate(flops=count * 6 * 10**9, bytes_accessed=6 * 10**6, transcendentals=0),
        name=f"near{block}",
    )(a, b, c, src, cls, maps)


def halo_body(below_ref, above_ref, up_ref, out_ref, stack):
    children = jnp.concatenate([below_ref[...], above_ref[...]], axis=1)
    out_ref[...] = ascend(children, up_ref, stack).astype(BF)


def halo_six(below, above, up):
    return pl.pallas_call(
        halo_body,
        out_shape=jax.ShapeDtypeStruct((F, 128), BF),
        in_specs=[VM] * 3,
        out_specs=VM,
        scratch_shapes=[pltpu.VMEM((8 * F, 128), F32)],
        compiler_params=pltpu.CompilerParams(vmem_limit_bytes=16 * 2**20),
        cost_estimate=pl.CostEstimate(flops=2 * 10**9, bytes_accessed=3 * 10**6, transcendentals=0),
        name="halo",
    )(below, above, up)


def flip_body(down_ref, out_ref):
    out_ref[...] = down_ref[...].T


def flip(down):
    return pl.pallas_call(
        flip_body,
        out_shape=jax.ShapeDtypeStruct((8 * F, F), BF),
        in_specs=[VM],
        out_specs=VM,
        compiler_params=pltpu.CompilerParams(vmem_limit_bytes=16 * 2**20),
        cost_estimate=pl.CostEstimate(flops=10**9, bytes_accessed=3 * 10**6, transcendentals=0),
        name="flip",
    )(down)


def last_body(
    t0, t1, t2, t3, t4, t5, t6, t7, index_ref, six_ref, halo_ref, src_ref, cls_ref, up_ref, down_ref,
    s0, s1, s2, maps_ref, out_ref,
    even, odd, grouped, stack, coarse, both, weave, fars, local,
):
    window = jnp.concatenate([six_ref[...], halo_ref[...]], axis=1)

    def pick(i, carry):
        wanted = jnp.concatenate([src_ref[pl.ds(2 * i, 1), :], src_ref[pl.ds(2 * i + 1, 1), :]], axis=1)
        value = dot(window, onehot(wanted, 256))
        for q in range(2):
            spread(value[:, 128 * q : 128 * q + 128], even, odd, 2 * i + q, slice(128, 256))
        return carry

    lax.fori_loop(0, LIST // 2, pick, 0)

    wanted = index_ref[...]
    picked = jnp.zeros((F, 256), F32)
    for k, table in enumerate((t0, t1, t2, t3, t4, t5, t6, t7)):
        picked += dot(table[...], onehot(wanted - 512 * k, 512))
    stack[...] = jnp.zeros(stack.shape, F32)
    for o in range(8):
        stack[o * F : (o + 1) * F, :16] = picked[:, 128 + 16 * o : 144 + 16 * o]
    four = dot(up_ref[...], stack[...].astype(BF)).astype(BF).astype(F32)
    blank = jnp.zeros((F, 110), F32)
    for j in range(LIST):
        value = jnp.concatenate([picked[:, 16 * j : 16 * j + 16], four[:, 2 * j : 2 * j + 2], blank], axis=1)
        spread(value, even, odd, j, slice(0, 128))

    def sums(p, carry):
        group([cls_ref[j : j + 1, :] for j in range(LIST)], even, odd, grouped, p)
        return carry

    lax.fori_loop(0, KINDS // 2, sums, 0)
    coarse[...] = dot(maps_ref[...], grouped[...])

    def fill(o, carry):
        row = lax.broadcasted_iota(jnp.int32, (128, 1024), 0)
        cell = lax.broadcasted_iota(jnp.int32, (128, 1024), 1)
        weave[pl.ds(pl.multiple_of(o * 128, 128), 128), :] = jnp.where(cell == 8 * row + o, 1.0, 0.0).astype(BF)
        return carry

    lax.fori_loop(0, 8, fill, 0)
    both[...] = jnp.zeros(both.shape, BF)
    lane = lax.broadcasted_iota(jnp.int32, (F, 128), 1)
    fars[0] = jnp.where(lane < 16, coarse[:, :128], 0.0)
    fars[1] = coarse[:, 128:]
    take = lax.broadcasted_iota(jnp.int32, (128, 128), 0) == lax.broadcasted_iota(jnp.int32, (128, 128), 1) + 16
    local[...] = dot(coarse[:, :128].astype(BF), jnp.where(take, 1.0, 0.0).astype(BF)).astype(BF)

    def woven(lanes):
        pieces = dot(both[...], weave[:, lanes])
        return pieces[:F, :] + pieces[304 : 304 + F, :]

    def fall(level, carry):
        children = dot(down_ref[...], local[...])
        for o in range(8):
            part = children[o * F : (o + 1) * F, :]
            high = part.astype(BF)
            both[:F, 128 * o : 128 * o + 128] = high
            both[304 : 304 + F, 128 * o : 128 * o + 128] = (part - high.astype(F32)).astype(BF)

        @pl.when(level < 2)
        def _():
            local[...] = (woven(slice(0, 128)) + fars[jnp.minimum(level, 1)]).astype(BF)

        return carry

    lax.fori_loop(0, 3, fall, 0)
    for q, seven in enumerate((s0.at[0], s1.at[0], s2.at[0], s2.at[1])):
        lanes = slice(256 * q, 256 * q + 256)
        out_ref[:, lanes] = (woven(lanes) + seven[...]).astype(BF)


def last(tables, index, six, halo, src, cls, up, down, sevens, maps):
    return pl.pallas_call(
        last_body,
        out_shape=jax.ShapeDtypeStruct((F, 1024), BF),
        in_specs=[VM] * 19,
        out_specs=VM,
        scratch_shapes=[
            pltpu.VMEM((LIST, F + 8, 256), BF),
            pltpu.VMEM((LIST, F + 8, 256), BF),
            pltpu.VMEM((KINDS * F, 256), BF),
            pltpu.VMEM((8 * F, 128), F32),
            pltpu.VMEM((F, 256), F32),
            pltpu.VMEM((608, 1024), BF),
            pltpu.VMEM((1024, 1024), BF),
            pltpu.VMEM((2, F, 128), F32),
            pltpu.VMEM((F, 128), BF),
        ],
        compiler_params=pltpu.CompilerParams(vmem_limit_bytes=24 * 2**20),
        cost_estimate=pl.CostEstimate(flops=8 * 10**9, bytes_accessed=12 * 10**6, transcendentals=0),
        name="last",
    )(*tables, index, six, halo, src, cls, up, down, *sevens, maps)


def shifted(value, axis, steps):
    count = lax.axis_size(axis)
    first, last_one = (max(0, -steps), min(count, count - steps))
    return lax.ppermute(value, axis, [(source, source + steps) for source in range(first, last_one)])


def turned(value, axis, size, stride, steps):
    pairs = []
    for source in range(lax.axis_size(axis)):
        position = (source // stride) % size
        target = source + ((position + steps) % size - position) * stride
        pairs.append((source, target))
    return lax.ppermute(value, axis, pairs)


along_z = lambda value, steps: turned(value, "cells", 8, 8, steps)
along_y = lambda value, steps: turned(value, "cells", 4, 2, steps)
along_core = lambda value, steps: turned(value, "cells", 2, 1, steps)
along_x = lambda value, steps: turned(value, "sub", 4, 1, steps)


def tie(*values):
    return lax.optimization_barrier(values)


def body(
    leaf_multipoles,
    occupancy,
    upward_maps,
    transfer_maps,
    downward_maps,
    sources_seven,
    classes_seven,
    sources_six,
    classes_six,
    sources_five,
    classes_five,
    sources_four,
    classes_four,
):
    leaves = leaf_multipoles.T
    up, maps = upward_maps.T, transfer_maps.T
    masked = leaves * occupancy.astype(BF)[None, :]
    lo, hi = masked[:, :512], masked[:, 512:]
    below = shifted(hi, ("cells", "sub"), 1)
    above = shifted(lo, ("cells", "sub"), -1)
    six, five = rise(lo, hi, up)

    cells, sub = lax.axis_index("cells"), lax.axis_index("sub")
    place = cells * 4 + sub
    src_seven = sources_seven.T - (place * 1024 - 512)
    cls_seven = classes_seven.T
    rel_six = sources_six.T - (place * 128 - 64)
    src_six = jnp.where(rel_six < 64, rel_six + 128, jnp.where(rel_six < 192, rel_six - 64, rel_six))

    down = flip(downward_maps)
    minus, plus = along_z(five, 1), along_z(five, -1)
    three = jnp.stack([minus, five, plus])
    three, near_lo = tie(three, lo)
    upper = along_z(three, -3)
    lower = along_z(three[1:], 3)
    seven_0 = near(0, 1, below, near_lo, hi, src_seven, cls_seven, maps)
    lower, upper, seven_0 = tie(lower, upper, seven_0)
    column = jnp.concatenate([lower, three, upper], axis=0).reshape(128, F).T
    column, seven_0, near_lo = tie(column, seven_0, near_lo)
    sides = along_y(column, -1), along_y(column, 2), along_y(column, 1)
    seven_1 = near(1, 1, below, near_lo, hi, src_seven, cls_seven, maps)
    *sides, seven_1 = tie(*sides, seven_1)
    plane = jnp.concatenate([column, *sides], axis=1)
    plane, seven_1, near_lo, near_up = tie(plane, seven_1, near_lo, up)
    tables = [plane, along_x(plane, -1), along_x(plane, 2), along_x(plane, 1)]
    halo = halo_six(below, above, near_up)
    seven_2 = near(2, 2, near_lo, hi, above, src_seven, cls_seven, maps)
    *tables, seven_2, halo = tie(*tables, seven_2, halo)
    tables = tables + [along_core(table, 1) for table in tables]
    sevens = [seven_0, seven_1, seven_2]

    def where_held(cell):
        device = cell // 16
        there = (device // 4, device % 4)
        dz = (there[0] // 8 - cells // 8 + 3) % 8
        dy = (there[0] // 2 - cells // 2) % 4
        dc = (there[0] - cells) % 2
        dx = (there[1] - sub) % 4
        return (dc * 4 + dx) * 512 + dy * 128 + dz * 16 + cell % 16

    entries_five = sources_five.T.reshape(1, 128)
    entries_four = sources_four.T.reshape(1, 16)
    octants = jnp.arange(8, dtype=jnp.int32)[:, None]
    children = (8 * entries_four + octants).reshape(1, 128)
    index = where_held(jnp.concatenate([entries_five, children], axis=1))
    cls_low = jnp.concatenate(
        [classes_five.T, classes_four.T, jnp.full((LIST, 110), KINDS, jnp.int32), classes_six.T], axis=1
    )
    return last(tables, index, six, halo, src_six, cls_low, up, down, sevens, maps).T


def solution(mesh):
    in_specs = (
        P(("cells", "sub"), None),
        P(("cells", "sub")),
        P(),
        P(),
        P(),
        P(("cells", "sub"), None),
        P(("cells", "sub"), None),
        P(("cells", "sub"), None),
        P(("cells", "sub"), None),
        P(("cells", "sub"), None),
        P(("cells", "sub"), None),
        P(("cells", "sub"), None),
        P(("cells", "sub"), None),
    )
    out_specs = P(("cells", "sub"), None)
    return jax.shard_map(body, mesh=mesh, in_specs=in_specs, out_specs=out_specs, check_vma=False)
```

```python
import functools

import jax
import jax.numpy as jnp
from jax import lax
from jax.experimental import pallas as pl
from jax.experimental.pallas import tpu as pltpu
from jax.sharding import PartitionSpec as P

F = 296
KINDS = 32
LIST = 8
BF = jnp.bfloat16
F32 = jnp.float32
VM = pl.BlockSpec(memory_space=pltpu.VMEM)


def place():
    return lax.axis_index("cells") * 4 + lax.axis_index("sub")


def dot(a, b):
    return jnp.dot(a, b, preferred_element_type=F32)


def onehot(rel, depth):
    count = rel.shape[1]
    rows = lax.broadcasted_iota(jnp.int32, (depth, count), 0)
    return jnp.where(rows == rel, 1.0, 0.0).astype(BF)


def split_octants(children, first, width):
    count = children.shape[1]
    source = lax.broadcasted_iota(jnp.int32, (count, 2 * width), 0)
    place = lax.broadcasted_iota(jnp.int32, (count, 2 * width), 1)
    second = (place >= width).astype(jnp.int32)
    wanted = 8 * (place - width * second) + first + second
    return dot(children, jnp.where(source == wanted, 1.0, 0.0).astype(BF))


def ascend(children, up_ref, stack):
    for pair in range(4):
        both = split_octants(children, 2 * pair, 128)
        stack[2 * pair * F : (2 * pair + 1) * F, :] = both[:, :128]
        stack[(2 * pair + 1) * F : (2 * pair + 2) * F, :] = both[:, 128:]
    return dot(up_ref[...], stack[...].astype(BF))


def rise_body(lo_ref, hi_ref, up_ref, six_ref, five_ref, stack):
    children = jnp.concatenate([lo_ref[...], hi_ref[...]], axis=1)
    six = ascend(children, up_ref, stack).astype(BF)
    six_ref[...] = six
    five = ascend(six, up_ref, stack)
    five_ref[...] = five.T[:16, :].astype(BF)


def rise(lo, hi, up):
    return pl.pallas_call(
        rise_body,
        out_shape=(
            jax.ShapeDtypeStruct((F, 128), BF),
            jax.ShapeDtypeStruct((16, F), BF),
        ),
        in_specs=[VM] * 3,
        out_specs=(VM,) * 2,
        scratch_shapes=[pltpu.VMEM((8 * F, 128), F32)],
        compiler_params=pltpu.CompilerParams(vmem_limit_bytes=16 * 2**20),
        cost_estimate=pl.CostEstimate(flops=8 * 10**9, bytes_accessed=3 * 10**6, transcendentals=0),
        name="rise",
    )(lo, hi, up)


def spread(value, even, odd, slot, lanes):
    blank = jnp.zeros((8, value.shape[1]), F32)
    even[slot, :, lanes] = jnp.concatenate([value, blank], axis=0).astype(BF)
    odd[slot, :, lanes] = jnp.concatenate([blank, value], axis=0).astype(BF)


def stack_pair(grouped, row, lanes, even_tile, odd_tile):
    for i in range(18):
        grouped[pl.ds(row + 16 * i, 16), lanes] = even_tile(i)
    grouped[pl.ds(row + 288, 16), lanes] = even_tile(18) + odd_tile(0)
    for i in range(1, 19):
        grouped[pl.ds(row + 288 + 16 * i, 16), lanes] = odd_tile(i)


def group(labels, even, odd, grouped, p):
    wide = [jnp.broadcast_to(label, (16, 256)) for label in labels]

    def masks(kind):
        return [jnp.where(label == kind, 1.0, 0.0).astype(BF) for label in wide]

    first, second = masks(2 * p), masks(2 * p + 1)

    def total(ref, mask, i):
        terms = [ref[j, 16 * i : 16 * i + 16, :] * mask[j] for j in range(LIST)]
        while len(terms) > 1:
            terms = [terms[q] + terms[q + 1] for q in range(0, len(terms), 2)]
        return terms[0]

    stack_pair(
        grouped,
        pl.multiple_of(p * 2 * F, 16),
        slice(None),
        lambda i: total(even, first, i),
        lambda i: total(odd, second, i),
    )


def near_body(block, count, a_ref, b_ref, c_ref, src_ref, cls_ref, maps_ref, out_ref, window, even, odd, grouped):
    side = block % 2
    for k in range(4 + count):
        half = k + side
        window[:, 256 * k : 256 * k + 256] = (a_ref, b_ref, c_ref)[half // 2][:, 256 * (half % 2) : 256 * (half % 2) + 256]

    def pick(i, carry):
        local, four = i // 2, i % 2
        base = pl.multiple_of(local * 256, 256)
        lanes = pl.ds(pl.multiple_of((block + local) * 256, 256), 256)
        start = place() * 1024 - 512 + (block + local) * 256
        wanted = [onehot(src_ref[pl.ds(4 * four + q, 1), lanes] - start, 1280) for q in range(4)]
        value = dot(window[:, pl.ds(base, 1280)], jnp.concatenate(wanted, axis=1))
        for q in range(4):
            spread(value[:, 256 * q : 256 * q + 256], even.at[local], odd.at[local], 4 * four + q, slice(None))
        return carry

    lax.fori_loop(0, 2 * count, pick, 0)

    def sums(i, carry):
        local, p = i // 16, i % 16
        lanes = pl.ds(pl.multiple_of((block + local) * 256, 256), 256)
        labels = [cls_ref[j : j + 1, lanes] for j in range(LIST)]
        group(labels, even.at[local], odd.at[local], grouped.at[local], p)
        return carry

    lax.fori_loop(0, 16 * count, sums, 0)

    def send(i, carry):
        out_ref[i] = dot(maps_ref[...], grouped[i])
        return carry

    lax.fori_loop(0, count, send, 0)


def near(block, count, a, b, c, src, cls, maps):
    return pl.pallas_call(
        functools.partial(near_body, block, count),
        out_shape=jax.ShapeDtypeStruct((count, F, 256), F32),
        in_specs=[VM] * 6,
        out_specs=VM,
        scratch_shapes=[
            pltpu.VMEM((F, 1024 + 256 * count), BF),
            pltpu.VMEM((count, LIST, F + 8, 256), BF),
            pltpu.VMEM((count, LIST, F + 8, 256), BF),
            pltpu.VMEM((count, KINDS * F, 256), BF),
        ],
        compiler_params=pltpu.CompilerParams(vmem_limit_bytes=(22 if count > 1 else 16) * 2**20),
        cost_estimate=pl.CostEstimate(flops=count * 6 * 10**9, bytes_accessed=6 * 10**6, transcendentals=0),
        name=f"near{block}",
    )(a, b, c, src, cls, maps)


def turn_body(lower_ref, middle_ref, upper_ref, out_ref):
    parts = [ref[k].astype(F32) for ref in (lower_ref, middle_ref, upper_ref) for k in range(ref.shape[0])]
    out_ref[...] = jnp.concatenate(parts, axis=0).T.astype(BF)


def turn(lower, three, upper):
    return pl.pallas_call(
        turn_body,
        out_shape=jax.ShapeDtypeStruct((F, 128), BF),
        in_specs=[VM] * 3,
        out_specs=VM,
        compiler_params=pltpu.CompilerParams(vmem_limit_bytes=8 * 2**20),
        cost_estimate=pl.CostEstimate(flops=10**8, bytes_accessed=10**5, transcendentals=0),
        name="turn",
    )(lower, three, upper)


def halo_body(below_ref, above_ref, up_ref, out_ref, stack):
    children = jnp.concatenate([below_ref[...], above_ref[...]], axis=1)
    out_ref[...] = ascend(children, up_ref, stack).astype(BF)


def halo_six(below, above, up):
    return pl.pallas_call(
        halo_body,
        out_shape=jax.ShapeDtypeStruct((F, 128), BF),
        in_specs=[VM] * 3,
        out_specs=VM,
        scratch_shapes=[pltpu.VMEM((8 * F, 128), F32)],
        compiler_params=pltpu.CompilerParams(vmem_limit_bytes=16 * 2**20),
        cost_estimate=pl.CostEstimate(flops=2 * 10**9, bytes_accessed=3 * 10**6, transcendentals=0),
        name="halo",
    )(below, above, up)


def flip_body(down_ref, out_ref):
    out_ref[...] = down_ref[...].T


def flip(down):
    return pl.pallas_call(
        flip_body,
        out_shape=jax.ShapeDtypeStruct((8 * F, F), BF),
        in_specs=[VM],
        out_specs=VM,
        compiler_params=pltpu.CompilerParams(vmem_limit_bytes=16 * 2**20),
        cost_estimate=pl.CostEstimate(flops=10**9, bytes_accessed=3 * 10**6, transcendentals=0),
        name="flip",
    )(down)


def where_held(cell):
    cells, sub = lax.axis_index("cells"), lax.axis_index("sub")
    there = cell >> 6
    dz = ((there >> 3) - (cells >> 3) + 3) & 7
    dy = ((there >> 1) - (cells >> 1)) & 3
    dc = (there - cells) & 1
    dx = ((cell >> 4) - sub) & 3
    return (dc * 4 + dx) * 512 + dy * 128 + dz * 16 + (cell & 15)


def last_body(
    t0, t1, t2, t3, t4, t5, t6, t7, six_ref, halo_ref, src6_ref, cls6_ref, src5_ref, cls5_ref, src4_ref, cls4_ref,
    up_ref, down_ref,
    s0, s1, s2, maps_ref, out_ref,
    even, odd, grouped, stack, coarse, both, weave, fars, local, src_ref, cls_ref,
):
    window = jnp.concatenate([six_ref[...], halo_ref[...]], axis=1)
    rel = src6_ref[...] - (place() * 128 - 64)
    src_ref[...] = jnp.where(rel < 64, rel + 128, jnp.where(rel < 192, rel - 64, rel))
    entry = lax.broadcasted_iota(jnp.int32, (8, 8), 0)
    column = lax.broadcasted_iota(jnp.int32, (8, 8), 1)
    four_labels = [
        jnp.sum(jnp.where(entry == column, cls4_ref[t : t + 1, :], 0).astype(F32), axis=1, keepdims=True)
        for t in range(2)
    ]
    unused = jnp.full((8, 110), KINDS, jnp.int32)
    cls_ref[:, :128] = jnp.concatenate([cls5_ref[...], *(x.astype(jnp.int32) for x in four_labels), unused], axis=1)
    cls_ref[:, 128:] = cls6_ref[...]

    def pick(i, carry):
        wanted = jnp.concatenate([src_ref[pl.ds(2 * i, 1), :], src_ref[pl.ds(2 * i + 1, 1), :]], axis=1)
        value = dot(window, onehot(wanted, 256))
        for q in range(2):
            spread(value[:, 128 * q : 128 * q + 128], even, odd, 2 * i + q, slice(128, 256))
        return carry

    lax.fori_loop(0, LIST // 2, pick, 0)

    entries_four = jnp.concatenate([src4_ref[0:1, :], src4_ref[1:2, :]], axis=1)
    wanted = jnp.concatenate(
        [src5_ref[j : j + 1, :] for j in range(LIST)] + [8 * entries_four + o for o in range(8)], axis=1
    )
    wanted = where_held(wanted)
    picked = jnp.zeros((F, 256), F32)
    for k, table in enumerate((t0, t1, t2, t3, t4, t5, t6, t7)):
        picked += dot(table[...], onehot(wanted - 512 * k, 512))
    stack[...] = jnp.zeros(stack.shape, F32)
    for o in range(8):
        stack[o * F : (o + 1) * F, :16] = picked[:, 128 + 16 * o : 144 + 16 * o]
    four = dot(up_ref[...], stack[...].astype(BF)).astype(BF).astype(F32)
    blank = jnp.zeros((F, 110), F32)
    for j in range(LIST):
        value = jnp.concatenate([picked[:, 16 * j : 16 * j + 16], four[:, j : j + 1], four[:, 8 + j : 9 + j], blank], axis=1)
        spread(value, even, odd, j, slice(0, 128))

    def sums(p, carry):
        group([cls_ref[j : j + 1, :] for j in range(LIST)], even, odd, grouped, p)
        return carry

    lax.fori_loop(0, KINDS // 2, sums, 0)
    coarse[...] = dot(maps_ref[...], grouped[...])

    def fill(o, carry):
        row = lax.broadcasted_iota(jnp.int32, (128, 1024), 0)
        cell = lax.broadcasted_iota(jnp.int32, (128, 1024), 1)
        weave[pl.ds(pl.multiple_of(o * 128, 128), 128), :] = jnp.where(cell == 8 * row + o, 1.0, 0.0).astype(BF)
        return carry

    lax.fori_loop(0, 8, fill, 0)
    both[...] = jnp.zeros(both.shape, BF)
    lane = lax.broadcasted_iota(jnp.int32, (F, 128), 1)
    fars[0] = jnp.where(lane < 16, coarse[:, :128], 0.0)
    fars[1] = coarse[:, 128:]
    take = lax.broadcasted_iota(jnp.int32, (128, 128), 0) == lax.broadcasted_iota(jnp.int32, (128, 128), 1) + 16
    local[...] = dot(coarse[:, :128].astype(BF), jnp.where(take, 1.0, 0.0).astype(BF)).astype(BF)

    def woven(lanes):
        pieces = dot(both[...], weave[:, lanes])
        return pieces[:F, :] + pieces[304 : 304 + F, :]

    def fall(level, carry):
        children = dot(down_ref[...], local[...])
        for o in range(8):
            part = children[o * F : (o + 1) * F, :]
            high = part.astype(BF)
            both[:F, 128 * o : 128 * o + 128] = high
            both[304 : 304 + F, 128 * o : 128 * o + 128] = (part - high.astype(F32)).astype(BF)

        @pl.when(level < 2)
        def _():
            local[...] = (woven(slice(0, 128)) + fars[jnp.minimum(level, 1)]).astype(BF)

        return carry

    lax.fori_loop(0, 3, fall, 0)
    for q, seven in enumerate((s0.at[0], s1.at[0], s2.at[0], s2.at[1])):
        lanes = slice(256 * q, 256 * q + 256)
        out_ref[:, lanes] = (woven(lanes) + seven[...]).astype(BF)


def last(tables, six, halo, lists, up, down, sevens, maps):
    return pl.pallas_call(
        last_body,
        out_shape=jax.ShapeDtypeStruct((F, 1024), BF),
        in_specs=[VM] * 22,
        out_specs=VM,
        scratch_shapes=[
            pltpu.VMEM((LIST, F + 8, 256), BF),
            pltpu.VMEM((LIST, F + 8, 256), BF),
            pltpu.VMEM((KINDS * F, 256), BF),
            pltpu.VMEM((8 * F, 128), F32),
            pltpu.VMEM((F, 256), F32),
            pltpu.VMEM((608, 1024), BF),
            pltpu.VMEM((1024, 1024), BF),
            pltpu.VMEM((2, F, 128), F32),
            pltpu.VMEM((F, 128), BF),
            pltpu.VMEM((LIST, 128), jnp.int32),
            pltpu.VMEM((LIST, 256), jnp.int32),
        ],
        compiler_params=pltpu.CompilerParams(vmem_limit_bytes=24 * 2**20),
        cost_estimate=pl.CostEstimate(flops=8 * 10**9, bytes_accessed=12 * 10**6, transcendentals=0),
        name="last",
    )(*tables, six, halo, *lists, up, down, *sevens, maps)


def shifted(value, axis, steps):
    count = lax.axis_size(axis)
    first, last_one = (max(0, -steps), min(count, count - steps))
    return lax.ppermute(value, axis, [(source, source + steps) for source in range(first, last_one)])


def turned(value, axis, size, stride, steps):
    pairs = []
    for source in range(lax.axis_size(axis)):
        position = (source // stride) % size
        target = source + ((position + steps) % size - position) * stride
        pairs.append((source, target))
    return lax.ppermute(value, axis, pairs)


along_z = lambda value, steps: turned(value, "cells", 8, 8, steps)
along_y = lambda value, steps: turned(value, "cells", 4, 2, steps)
along_core = lambda value, steps: turned(value, "cells", 2, 1, steps)
along_x = lambda value, steps: turned(value, "sub", 4, 1, steps)


def tie(*values):
    return lax.optimization_barrier(values)


def body(
    leaf_multipoles,
    occupancy,
    upward_maps,
    transfer_maps,
    downward_maps,
    sources_seven,
    classes_seven,
    sources_six,
    classes_six,
    sources_five,
    classes_five,
    sources_four,
    classes_four,
):
    leaves = leaf_multipoles.T
    up, maps = upward_maps.T, transfer_maps.T
    masked = leaves * occupancy.astype(BF)[None, :]
    lo, hi = masked[:, :512], masked[:, 512:]
    below = shifted(hi, ("cells", "sub"), 1)
    above = shifted(lo, ("cells", "sub"), -1)
    six, five = rise(lo, hi, up)

    src_seven, cls_seven = sources_seven.T, classes_seven.T

    down = flip(downward_maps)
    minus, plus = along_z(five, 1), along_z(five, -1)
    three = jnp.stack([minus, five, plus])
    three, near_lo = tie(three, lo)
    upper = along_z(three, -3)
    lower = along_z(three[1:], 3)
    seven_0 = near(0, 1, below, near_lo, hi, src_seven, cls_seven, maps)
    lower, upper, seven_0 = tie(lower, upper, seven_0)
    column = turn(lower, three, upper)
    column, seven_0, near_lo = tie(column, seven_0, near_lo)
    sides = along_y(column, -1), along_y(column, 2), along_y(column, 1)
    seven_1 = near(1, 1, below, near_lo, hi, src_seven, cls_seven, maps)
    *sides, seven_1 = tie(*sides, seven_1)
    plane = jnp.concatenate([column, *sides], axis=1)
    plane, seven_1, near_lo, near_up = tie(plane, seven_1, near_lo, up)
    tables = [plane, along_x(plane, -1), along_x(plane, 2), along_x(plane, 1)]
    halo = halo_six(below, above, near_up)
    seven_2 = near(2, 2, near_lo, hi, above, src_seven, cls_seven, maps)
    *tables, seven_2, halo = tie(*tables, seven_2, halo)
    tables = tables + [along_core(table, 1) for table in tables]
    sevens = [seven_0, seven_1, seven_2]

    lists = (
        sources_six.T,
        classes_six.T,
        sources_five.T,
        classes_five.T,
        sources_four,
        classes_four,
    )
    return last(tables, six, halo, lists, up, down, sevens, maps).T


def solution(mesh):
    in_specs = (
        P(("cells", "sub"), None),
        P(("cells", "sub")),
        P(),
        P(),
        P(),
        P(("cells", "sub"), None),
        P(("cells", "sub"), None),
        P(("cells", "sub"), None),
        P(("cells", "sub"), None),
        P(("cells", "sub"), None),
        P(("cells", "sub"), None),
        P(("cells", "sub"), None),
        P(("cells", "sub"), None),
    )
    out_specs = P(("cells", "sub"), None)
    return jax.shard_map(body, mesh=mesh, in_specs=in_specs, out_specs=out_specs, check_vma=False)
```

```python
import functools

import jax
import jax.numpy as jnp
from jax import lax
from jax.experimental import pallas as pl
from jax.experimental.pallas import tpu as pltpu
from jax.sharding import PartitionSpec as P

F = 296
KINDS = 32
LIST = 8
BF = jnp.bfloat16
F32 = jnp.float32
VM = pl.BlockSpec(memory_space=pltpu.VMEM)


def place():
    return lax.axis_index("cells") * 4 + lax.axis_index("sub")


def dot(a, b):
    return jnp.dot(a, b, preferred_element_type=F32)


def onehot(rel, depth):
    count = rel.shape[1]
    rows = lax.broadcasted_iota(jnp.int32, (depth, count), 0)
    return jnp.where(rows == rel, 1.0, 0.0).astype(BF)


def split_octants(children, first, width):
    count = children.shape[1]
    source = lax.broadcasted_iota(jnp.int32, (count, 2 * width), 0)
    place_in = lax.broadcasted_iota(jnp.int32, (1, 2 * width), 1)
    second = (place_in >= width).astype(jnp.int32)
    wanted = 8 * (place_in - width * second) + first + second
    return dot(children, jnp.where(source == wanted, 1.0, 0.0).astype(BF))


def ascend(children, up_ref, stack):
    for pair in range(4):
        both = split_octants(children, 2 * pair, 128)
        stack[2 * pair * F : (2 * pair + 1) * F, :] = both[:, :128]
        stack[(2 * pair + 1) * F : (2 * pair + 2) * F, :] = both[:, 128:]
    return dot(up_ref[...], stack[...].astype(BF))


def rise_body(lo_ref, hi_ref, up_ref, six_ref, five_ref, stack):
    children = jnp.concatenate([lo_ref[...], hi_ref[...]], axis=1)
    six = ascend(children, up_ref, stack).astype(BF)
    six_ref[...] = six
    five = ascend(six, up_ref, stack)
    five_ref[...] = five.T[:16, :].astype(BF)


def rise(lo, hi, up):
    return pl.pallas_call(
        rise_body,
        out_shape=(
            jax.ShapeDtypeStruct((F, 128), BF),
            jax.ShapeDtypeStruct((16, F), BF),
        ),
        in_specs=[VM] * 3,
        out_specs=(VM,) * 2,
        scratch_shapes=[pltpu.VMEM((8 * F, 128), F32)],
        compiler_params=pltpu.CompilerParams(vmem_limit_bytes=16 * 2**20),
        cost_estimate=pl.CostEstimate(flops=8 * 10**9, bytes_accessed=3 * 10**6, transcendentals=0),
        name="rise",
    )(lo, hi, up)


def spread(value, even, odd, slot, lanes):
    blank = jnp.zeros((8, value.shape[1]), F32)
    even[slot, :, lanes] = jnp.concatenate([value, blank], axis=0).astype(BF)
    odd[slot, :, lanes] = jnp.concatenate([blank, value], axis=0).astype(BF)


def stack_pair(grouped, row, lanes, even_tile, odd_tile):
    for i in range(18):
        grouped[pl.ds(row + 16 * i, 16), lanes] = even_tile(i)
    grouped[pl.ds(row + 288, 16), lanes] = even_tile(18) + odd_tile(0)
    for i in range(1, 19):
        grouped[pl.ds(row + 288 + 16 * i, 16), lanes] = odd_tile(i)


def prepare(labels, wide):
    for j in range(LIST):
        wide[j] = jnp.broadcast_to(labels[j : j + 1, :].astype(F32), (16, 256)).astype(BF)


def group(wide, even, odd, grouped, p, few=0):
    def masks(kind):
        wanted = jnp.full((16, 256), kind, F32).astype(BF)
        return [jnp.where(wide[j] == wanted, jnp.ones((), BF), jnp.zeros((), BF)) for j in range(LIST)]

    first, second = masks(2 * p), masks(2 * p + 1)

    def part(ref, mask, i, count, lanes):
        terms = [ref[j, 16 * i : 16 * i + 16, lanes] * mask[j][:, lanes] for j in range(count)]
        while len(terms) > 1:
            terms = [terms[q] + terms[q + 1] for q in range(0, len(terms), 2)]
        return terms[0]

    def total(ref, mask, i):
        if not few:
            return part(ref, mask, i, LIST, slice(None))
        low = part(ref, mask, i, few, slice(0, 128))
        return jnp.concatenate([low, part(ref, mask, i, LIST, slice(128, 256))], axis=1)

    stack_pair(
        grouped,
        pl.multiple_of(p * 2 * F, 16),
        slice(None),
        lambda i: total(even, first, i),
        lambda i: total(odd, second, i),
    )


def near_body(block, count, a_ref, b_ref, c_ref, src_ref, cls_ref, maps_ref, out_ref, window, even, odd, grouped, wide):
    side = block % 2
    for k in range(4 + count):
        half = k + side
        window[:, 256 * k : 256 * k + 256] = (a_ref, b_ref, c_ref)[half // 2][:, 256 * (half % 2) : 256 * (half % 2) + 256]

    def pick(i, carry):
        local, four = i // 2, i % 2
        base = pl.multiple_of(local * 256, 256)
        lanes = pl.ds(pl.multiple_of((block + local) * 256, 256), 256)
        start = place() * 1024 - 512 + (block + local) * 256
        wanted = [onehot(src_ref[pl.ds(4 * four + q, 1), lanes] - start, 1280) for q in range(4)]
        value = dot(window[:, pl.ds(base, 1280)], jnp.concatenate(wanted, axis=1))
        for q in range(4):
            spread(value[:, 256 * q : 256 * q + 256], even.at[local], odd.at[local], 4 * four + q, slice(None))
        return carry

    lax.fori_loop(0, 2 * count, pick, 0)

    def sums(i, carry):
        local, p = i // 16, i % 16
        lanes = pl.ds(pl.multiple_of((block + local) * 256, 256), 256)
        pl.when(p == 0)(lambda: prepare(cls_ref[:, lanes], wide))
        group(wide, even.at[local], odd.at[local], grouped.at[local], p)
        return carry

    lax.fori_loop(0, 16 * count, sums, 0)

    def send(i, carry):
        out_ref[i] = dot(maps_ref[...], grouped[i])
        return carry

    lax.fori_loop(0, count, send, 0)


def near(block, count, a, b, c, src, cls, maps):
    return pl.pallas_call(
        functools.partial(near_body, block, count),
        out_shape=jax.ShapeDtypeStruct((count, F, 256), F32),
        in_specs=[VM] * 6,
        out_specs=VM,
        scratch_shapes=[
            pltpu.VMEM((F, 1024 + 256 * count), BF),
            pltpu.VMEM((count, LIST, F + 8, 256), BF),
            pltpu.VMEM((count, LIST, F + 8, 256), BF),
            pltpu.VMEM((count, KINDS * F, 256), BF),
            pltpu.VMEM((LIST, 16, 256), BF),
        ],
        compiler_params=pltpu.CompilerParams(vmem_limit_bytes=(22 if count > 1 else 16) * 2**20),
        cost_estimate=pl.CostEstimate(flops=count * 6 * 10**9, bytes_accessed=6 * 10**6, transcendentals=0),
        name=f"near{block}",
    )(a, b, c, src, cls, maps)


def turn_body(lower_ref, middle_ref, upper_ref, out_ref):
    parts = [ref[k].astype(F32) for ref in (lower_ref, middle_ref, upper_ref) for k in range(ref.shape[0])]
    out_ref[...] = jnp.concatenate(parts, axis=0).T.astype(BF)


def turn(lower, three, upper):
    return pl.pallas_call(
        turn_body,
        out_shape=jax.ShapeDtypeStruct((F, 128), BF),
        in_specs=[VM] * 3,
        out_specs=VM,
        compiler_params=pltpu.CompilerParams(vmem_limit_bytes=8 * 2**20),
        cost_estimate=pl.CostEstimate(flops=10**8, bytes_accessed=10**5, transcendentals=0),
        name="turn",
    )(lower, three, upper)


def halo_body(below_ref, above_ref, up_ref, out_ref, stack):
    children = jnp.concatenate([below_ref[...], above_ref[...]], axis=1)
    out_ref[...] = ascend(children, up_ref, stack).astype(BF)


def halo_six(below, above, up):
    return pl.pallas_call(
        halo_body,
        out_shape=jax.ShapeDtypeStruct((F, 128), BF),
        in_specs=[VM] * 3,
        out_specs=VM,
        scratch_shapes=[pltpu.VMEM((8 * F, 128), F32)],
        compiler_params=pltpu.CompilerParams(vmem_limit_bytes=16 * 2**20),
        cost_estimate=pl.CostEstimate(flops=2 * 10**9, bytes_accessed=3 * 10**6, transcendentals=0),
        name="halo",
    )(below, above, up)


def flip_body(down_ref, out_ref):
    out_ref[...] = down_ref[...].T


def flip(down):
    return pl.pallas_call(
        flip_body,
        out_shape=jax.ShapeDtypeStruct((8 * F, F), BF),
        in_specs=[VM],
        out_specs=VM,
        compiler_params=pltpu.CompilerParams(vmem_limit_bytes=16 * 2**20),
        cost_estimate=pl.CostEstimate(flops=10**9, bytes_accessed=3 * 10**6, transcendentals=0),
        name="flip",
    )(down)


def where_held(cell):
    cells, sub = lax.axis_index("cells"), lax.axis_index("sub")
    there = cell >> 6
    dz = ((there >> 3) - (cells >> 3) + 3) & 7
    dy = ((there >> 1) - (cells >> 1)) & 3
    dc = (there - cells) & 1
    dx = ((cell >> 4) - sub) & 3
    return (dc * 4 + dx) * 512 + dy * 128 + dz * 16 + (cell & 15)


def last_body(
    t0, t1, t2, t3, t4, t5, t6, t7, six_ref, halo_ref, src6_ref, cls6_ref, src5_ref, cls5_ref, src4_ref, cls4_ref,
    up_ref, down_ref,
    s0, s1, s2, maps_ref, out_ref,
    even, odd, grouped, stack, coarse, both, weave, fars, local, src_ref, cls_ref, wide,
):
    window = jnp.concatenate([six_ref[...], halo_ref[...]], axis=1)
    rel = src6_ref[...] - (place() * 128 - 64)
    src_ref[...] = jnp.where(rel < 64, rel + 128, jnp.where(rel < 192, rel - 64, rel))
    cls_ref[...] = jnp.full((LIST, 256), KINDS, jnp.int32)
    for r in range(2):
        row = [cls5_ref[4 * r + j : 4 * r + j + 1, :] for j in range(4)]
        cls_ref[r : r + 1, :64] = jnp.concatenate(row, axis=1)
    cls_ref[0:1, 64:80] = jnp.concatenate([cls4_ref[0:1, :], cls4_ref[1:2, :]], axis=1)
    cls_ref[:, 128:] = cls6_ref[...]

    def pick(i, carry):
        wanted = jnp.concatenate([src_ref[pl.ds(2 * i, 1), :], src_ref[pl.ds(2 * i + 1, 1), :]], axis=1)
        value = dot(window, onehot(wanted, 256))
        for q in range(2):
            spread(value[:, 128 * q : 128 * q + 128], even, odd, 2 * i + q, slice(128, 256))
        return carry

    lax.fori_loop(0, LIST // 2, pick, 0)

    entries_four = jnp.concatenate([src4_ref[0:1, :], src4_ref[1:2, :]], axis=1)
    wanted = jnp.concatenate(
        [src5_ref[j : j + 1, :] for j in range(LIST)] + [8 * entries_four + o for o in range(8)], axis=1
    )
    wanted = where_held(wanted)
    picked = jnp.zeros((F, 256), F32)
    for k, table in enumerate((t0, t1, t2, t3, t4, t5, t6, t7)):
        picked += dot(table[...], onehot(wanted - 512 * k, 512))
    stack[...] = jnp.zeros(stack.shape, F32)
    for o in range(8):
        stack[o * F : (o + 1) * F, :16] = picked[:, 128 + 16 * o : 144 + 16 * o]
    four = dot(up_ref[...], stack[...].astype(BF)).astype(BF).astype(F32)
    low = slice(0, 128)
    spread(jnp.concatenate([picked[:, :64], four[:, :16], jnp.zeros((F, 48), F32)], axis=1), even, odd, 0, low)
    spread(jnp.concatenate([picked[:, 64:128], jnp.zeros((F, 64), F32)], axis=1), even, odd, 1, low)
    prepare(cls_ref[...], wide)

    def sums(p, carry):
        group(wide, even, odd, grouped, p, few=2)
        return carry

    lax.fori_loop(0, KINDS // 2, sums, 0)
    coarse[...] = dot(maps_ref[...], grouped[...])

    def fill(o, carry):
        parent = lax.broadcasted_iota(jnp.int32, (128, 1024), 0)
        cell = lax.broadcasted_iota(jnp.int32, (1, 1024), 1) - o
        cell = jnp.where((cell & 7) == 0, cell >> 3, -1)
        weave[pl.ds(pl.multiple_of(o * 128, 128), 128), :] = jnp.where(parent == cell, 1.0, 0.0).astype(BF)
        return carry

    lax.fori_loop(0, 8, fill, 0)
    both[...] = jnp.zeros(both.shape, BF)
    five = coarse[:, :16] + coarse[:, 16:32] + coarse[:, 32:48] + coarse[:, 48:64]
    fars[0] = jnp.concatenate([five, jnp.zeros((F, 112), F32)], axis=1)
    fars[1] = coarse[:, 128:]
    four = [jnp.sum(coarse[:, 64 + 8 * t : 72 + 8 * t], axis=1, keepdims=True) for t in range(2)]
    local[...] = jnp.concatenate([*four, jnp.zeros((F, 126), F32)], axis=1).astype(BF)

    def woven(lanes):
        pieces = dot(both[...], weave[:, lanes])
        return pieces[:F, :] + pieces[304 : 304 + F, :]

    def fall(level, carry):
        children = dot(down_ref[...], local[...])
        for o in range(8):
            part = children[o * F : (o + 1) * F, :]
            high = part.astype(BF)
            both[:F, 128 * o : 128 * o + 128] = high
            both[304 : 304 + F, 128 * o : 128 * o + 128] = (part - high.astype(F32)).astype(BF)

        @pl.when(level < 2)
        def _():
            local[...] = (woven(slice(0, 128)) + fars[jnp.minimum(level, 1)]).astype(BF)

        return carry

    lax.fori_loop(0, 3, fall, 0)
    for q, seven in enumerate((s0.at[0], s1.at[0], s2.at[0], s2.at[1])):
        lanes = slice(256 * q, 256 * q + 256)
        out_ref[:, lanes] = (woven(lanes) + seven[...]).astype(BF)


def last(tables, six, halo, lists, up, down, sevens, maps):
    return pl.pallas_call(
        last_body,
        out_shape=jax.ShapeDtypeStruct((F, 1024), BF),
        in_specs=[VM] * 22,
        out_specs=VM,
        scratch_shapes=[
            pltpu.VMEM((LIST, F + 8, 256), BF),
            pltpu.VMEM((LIST, F + 8, 256), BF),
            pltpu.VMEM((KINDS * F, 256), BF),
            pltpu.VMEM((8 * F, 128), F32),
            pltpu.VMEM((F, 256), F32),
            pltpu.VMEM((608, 1024), BF),
            pltpu.VMEM((1024, 1024), BF),
            pltpu.VMEM((2, F, 128), F32),
            pltpu.VMEM((F, 128), BF),
            pltpu.VMEM((LIST, 128), jnp.int32),
            pltpu.VMEM((LIST, 256), jnp.int32),
            pltpu.VMEM((LIST, 16, 256), BF),
        ],
        compiler_params=pltpu.CompilerParams(vmem_limit_bytes=24 * 2**20),
        cost_estimate=pl.CostEstimate(flops=8 * 10**9, bytes_accessed=12 * 10**6, transcendentals=0),
        name="last",
    )(*tables, six, halo, *lists, up, down, *sevens, maps)


def shifted(value, axis, steps):
    count = lax.axis_size(axis)
    first, last_one = (max(0, -steps), min(count, count - steps))
    return lax.ppermute(value, axis, [(source, source + steps) for source in range(first, last_one)])


def turned(value, axis, size, stride, steps):
    pairs = []
    for source in range(lax.axis_size(axis)):
        position = (source // stride) % size
        target = source + ((position + steps) % size - position) * stride
        pairs.append((source, target))
    return lax.ppermute(value, axis, pairs)


along_z = lambda value, steps: turned(value, "cells", 8, 8, steps)
along_y = lambda value, steps: turned(value, "cells", 4, 2, steps)
along_core = lambda value, steps: turned(value, "cells", 2, 1, steps)
along_x = lambda value, steps: turned(value, "sub", 4, 1, steps)


def tie(*values):
    return lax.optimization_barrier(values)


def body(
    leaf_multipoles,
    occupancy,
    upward_maps,
    transfer_maps,
    downward_maps,
    sources_seven,
    classes_seven,
    sources_six,
    classes_six,
    sources_five,
    classes_five,
    sources_four,
    classes_four,
):
    leaves = leaf_multipoles.T
    up, maps = upward_maps.T, transfer_maps.T
    masked = leaves * occupancy.astype(BF)[None, :]
    lo, hi = masked[:, :512], masked[:, 512:]
    below = shifted(hi, ("cells", "sub"), 1)
    above = shifted(lo, ("cells", "sub"), -1)
    six, five = rise(lo, hi, up)

    src_seven, cls_seven = sources_seven.T, classes_seven.T

    down = flip(downward_maps)
    minus, plus = along_z(five, 1), along_z(five, -1)
    three = jnp.stack([minus, five, plus])
    three, near_lo = tie(three, lo)
    upper = along_z(three, -3)
    lower = along_z(three[1:], 3)
    seven_0 = near(0, 1, below, near_lo, hi, src_seven, cls_seven, maps)
    lower, upper, seven_0 = tie(lower, upper, seven_0)
    column = turn(lower, three, upper)
    column, seven_0, near_lo = tie(column, seven_0, near_lo)
    sides = along_y(column, -1), along_y(column, 2), along_y(column, 1)
    seven_1 = near(1, 1, below, near_lo, hi, src_seven, cls_seven, maps)
    *sides, seven_1 = tie(*sides, seven_1)
    plane = jnp.concatenate([column, *sides], axis=1)
    plane, seven_1, near_lo, near_up = tie(plane, seven_1, near_lo, up)
    tables = [plane, along_x(plane, -1), along_x(plane, 2), along_x(plane, 1)]
    halo = halo_six(below, above, near_up)
    seven_2 = near(2, 2, near_lo, hi, above, src_seven, cls_seven, maps)
    *tables, seven_2, halo = tie(*tables, seven_2, halo)
    tables = tables + [along_core(table, 1) for table in tables]
    sevens = [seven_0, seven_1, seven_2]

    lists = (
        sources_six.T,
        classes_six.T,
        sources_five.T,
        classes_five.T,
        sources_four,
        classes_four,
    )
    return last(tables, six, halo, lists, up, down, sevens, maps).T


def solution(mesh):
    in_specs = (
        P(("cells", "sub"), None),
        P(("cells", "sub")),
        P(),
        P(),
        P(),
        P(("cells", "sub"), None),
        P(("cells", "sub"), None),
        P(("cells", "sub"), None),
        P(("cells", "sub"), None),
        P(("cells", "sub"), None),
        P(("cells", "sub"), None),
        P(("cells", "sub"), None),
        P(("cells", "sub"), None),
    )
    out_specs = P(("cells", "sub"), None)
    return jax.shard_map(body, mesh=mesh, in_specs=in_specs, out_specs=out_specs, check_vma=False)
```

```python
import functools

import jax
import jax.numpy as jnp
from jax import lax
from jax.experimental import pallas as pl
from jax.experimental.pallas import tpu as pltpu
from jax.sharding import PartitionSpec as P

F = 296
KINDS = 32
LIST = 8
BF = jnp.bfloat16
F32 = jnp.float32
VM = pl.BlockSpec(memory_space=pltpu.VMEM)


def place():
    return lax.axis_index("cells") * 4 + lax.axis_index("sub")


def dot(a, b):
    return jnp.dot(a, b, preferred_element_type=F32)


def onehot(rel, depth):
    count = rel.shape[1]
    rows = lax.broadcasted_iota(jnp.int32, (depth, count), 0)
    return jnp.where(rows == rel, 1.0, 0.0).astype(BF)


def split_octants(children, first, width):
    count = children.shape[1]
    source = lax.broadcasted_iota(jnp.int32, (count, 2 * width), 0)
    place = lax.broadcasted_iota(jnp.int32, (count, 2 * width), 1)
    second = (place >= width).astype(jnp.int32)
    wanted = 8 * (place - width * second) + first + second
    return dot(children, jnp.where(source == wanted, 1.0, 0.0).astype(BF))


def ascend(children, up_ref, stack):
    count = children.shape[1]
    source = lax.broadcasted_iota(jnp.int32, (count, 1024), 0)
    column = lax.broadcasted_iota(jnp.int32, (1, 1024), 1)
    both = dot(children, jnp.where(source == 8 * (column & 127) + (column >> 7), 1.0, 0.0).astype(BF))
    for o in range(8):
        stack[o * F : (o + 1) * F, :] = both[:, 128 * o : 128 * o + 128]
    return dot(up_ref[...], stack[...].astype(BF))


def rise_body(lo_ref, hi_ref, up_ref, six_ref, five_ref, stack):
    children = jnp.concatenate([lo_ref[...], hi_ref[...]], axis=1)
    six = ascend(children, up_ref, stack).astype(BF)
    six_ref[...] = six
    source = lax.broadcasted_iota(jnp.int32, (128, 128), 0)
    column = lax.broadcasted_iota(jnp.int32, (1, 128), 1)
    both = dot(six, jnp.where(source == 8 * (column & 15) + (column >> 4), 1.0, 0.0).astype(BF))
    for o in range(8):
        stack[o * F : (o + 1) * F, :16] = both[:, 16 * o : 16 * o + 16]
    five = dot(up_ref[...], stack[...].astype(BF))
    five_ref[...] = five.T[:16, :].astype(BF)


def rise(lo, hi, up):
    return pl.pallas_call(
        rise_body,
        out_shape=(
            jax.ShapeDtypeStruct((F, 128), BF),
            jax.ShapeDtypeStruct((16, F), BF),
        ),
        in_specs=[VM] * 3,
        out_specs=(VM,) * 2,
        scratch_shapes=[pltpu.VMEM((8 * F, 128), F32)],
        compiler_params=pltpu.CompilerParams(vmem_limit_bytes=16 * 2**20),
        cost_estimate=pl.CostEstimate(flops=8 * 10**9, bytes_accessed=3 * 10**6, transcendentals=0),
        name="rise",
    )(lo, hi, up)


def spread(value, even, odd, slot, lanes):
    blank = jnp.zeros((8, value.shape[1]), F32)
    even[slot, :, lanes] = jnp.concatenate([value, blank], axis=0).astype(BF)
    odd[slot, :, lanes] = jnp.concatenate([blank, value], axis=0).astype(BF)


def stack_pair(grouped, row, lanes, even_tile, odd_tile):
    for i in range(18):
        grouped[pl.ds(row + 16 * i, 16), lanes] = even_tile(i)
    grouped[pl.ds(row + 288, 16), lanes] = even_tile(18) + odd_tile(0)
    for i in range(1, 19):
        grouped[pl.ds(row + 288 + 16 * i, 16), lanes] = odd_tile(i)


def group(labels, even, odd, grouped, p):
    wide = [jnp.broadcast_to(label, (16, 256)) for label in labels]

    def masks(kind):
        return [jnp.where(label == kind, 1.0, 0.0).astype(BF) for label in wide]

    first, second = masks(2 * p), masks(2 * p + 1)

    def total(ref, mask, i):
        terms = [ref[j, 16 * i : 16 * i + 16, :] * mask[j] for j in range(LIST)]
        while len(terms) > 1:
            terms = [terms[q] + terms[q + 1] for q in range(0, len(terms), 2)]
        return terms[0]

    stack_pair(
        grouped,
        pl.multiple_of(p * 2 * F, 16),
        slice(None),
        lambda i: total(even, first, i),
        lambda i: total(odd, second, i),
    )


def near_body(block, count, a_ref, b_ref, c_ref, src_ref, cls_ref, maps_ref, out_ref, window, even, odd, grouped):
    side = block % 2
    for k in range(4 + count):
        half = k + side
        window[:, 256 * k : 256 * k + 256] = (a_ref, b_ref, c_ref)[half // 2][:, 256 * (half % 2) : 256 * (half % 2) + 256]

    def pick(i, carry):
        local, four = i // 2, i % 2
        base = pl.multiple_of(local * 256, 256)
        lanes = pl.ds(pl.multiple_of((block + local) * 256, 256), 256)
        start = place() * 1024 - 512 + (block + local) * 256
        wanted = [onehot(src_ref[pl.ds(4 * four + q, 1), lanes] - start, 1280) for q in range(4)]
        value = dot(window[:, pl.ds(base, 1280)], jnp.concatenate(wanted, axis=1))
        for q in range(4):
            spread(value[:, 256 * q : 256 * q + 256], even.at[local], odd.at[local], 4 * four + q, slice(None))
        return carry

    lax.fori_loop(0, 2 * count, pick, 0)

    def sums(i, carry):
        local, p = i // 16, i % 16
        lanes = pl.ds(pl.multiple_of((block + local) * 256, 256), 256)
        labels = [cls_ref[j : j + 1, lanes] for j in range(LIST)]
        group(labels, even.at[local], odd.at[local], grouped.at[local], p)
        return carry

    lax.fori_loop(0, 16 * count, sums, 0)

    def send(i, carry):
        out_ref[i] = dot(maps_ref[...], grouped[i])
        return carry

    lax.fori_loop(0, count, send, 0)


def near(block, count, a, b, c, src, cls, maps):
    return pl.pallas_call(
        functools.partial(near_body, block, count),
        out_shape=jax.ShapeDtypeStruct((count, F, 256), F32),
        in_specs=[VM] * 6,
        out_specs=VM,
        scratch_shapes=[
            pltpu.VMEM((F, 1024 + 256 * count), BF),
            pltpu.VMEM((count, LIST, F + 8, 256), BF),
            pltpu.VMEM((count, LIST, F + 8, 256), BF),
            pltpu.VMEM((count, KINDS * F, 256), BF),
        ],
        compiler_params=pltpu.CompilerParams(vmem_limit_bytes=(22 if count > 1 else 16) * 2**20),
        cost_estimate=pl.CostEstimate(flops=count * 6 * 10**9, bytes_accessed=6 * 10**6, transcendentals=0),
        name=f"near{block}",
    )(a, b, c, src, cls, maps)


def turn_body(lower_ref, middle_ref, upper_ref, out_ref):
    parts = [ref[k].astype(F32) for ref in (lower_ref, middle_ref, upper_ref) for k in range(ref.shape[0])]
    out_ref[...] = jnp.concatenate(parts, axis=0).T.astype(BF)


def turn(lower, three, upper):
    return pl.pallas_call(
        turn_body,
        out_shape=jax.ShapeDtypeStruct((F, 128), BF),
        in_specs=[VM] * 3,
        out_specs=VM,
        compiler_params=pltpu.CompilerParams(vmem_limit_bytes=8 * 2**20),
        cost_estimate=pl.CostEstimate(flops=10**8, bytes_accessed=10**5, transcendentals=0),
        name="turn",
    )(lower, three, upper)


def halo_body(below_ref, above_ref, up_ref, out_ref, stack):
    children = jnp.concatenate([below_ref[...], above_ref[...]], axis=1)
    out_ref[...] = ascend(children, up_ref, stack).astype(BF)


def halo_six(below, above, up):
    return pl.pallas_call(
        halo_body,
        out_shape=jax.ShapeDtypeStruct((F, 128), BF),
        in_specs=[VM] * 3,
        out_specs=VM,
        scratch_shapes=[pltpu.VMEM((8 * F, 128), F32)],
        compiler_params=pltpu.CompilerParams(vmem_limit_bytes=16 * 2**20),
        cost_estimate=pl.CostEstimate(flops=2 * 10**9, bytes_accessed=3 * 10**6, transcendentals=0),
        name="halo",
    )(below, above, up)


def flip_body(down_ref, out_ref):
    out_ref[...] = down_ref[...].T


def flip(down):
    return pl.pallas_call(
        flip_body,
        out_shape=jax.ShapeDtypeStruct((8 * F, F), BF),
        in_specs=[VM],
        out_specs=VM,
        compiler_params=pltpu.CompilerParams(vmem_limit_bytes=16 * 2**20),
        cost_estimate=pl.CostEstimate(flops=10**9, bytes_accessed=3 * 10**6, transcendentals=0),
        name="flip",
    )(down)


def where_held(cell):
    cells, sub = lax.axis_index("cells"), lax.axis_index("sub")
    there = cell >> 6
    dz = ((there >> 3) - (cells >> 3) + 3) & 7
    dy = ((there >> 1) - (cells >> 1)) & 3
    dc = (there - cells) & 1
    dx = ((cell >> 4) - sub) & 3
    return (dc * 4 + dx) * 512 + dy * 128 + dz * 16 + (cell & 15)


def last_body(
    t0, t1, t2, t3, t4, t5, t6, t7, six_ref, halo_ref, src6_ref, cls6_ref, src5_ref, cls5_ref, src4_ref, cls4_ref,
    up_ref, down_ref,
    s0, s1, s2, maps_ref, out_ref,
    even, odd, grouped, stack, coarse, both, weave, fars, local, src_ref, cls_ref,
):
    window = jnp.concatenate([six_ref[...], halo_ref[...]], axis=1)
    rel = src6_ref[...] - (place() * 128 - 64)
    src_ref[...] = jnp.where(rel < 64, rel + 128, jnp.where(rel < 192, rel - 64, rel))
    entry = lax.broadcasted_iota(jnp.int32, (8, 8), 0)
    column = lax.broadcasted_iota(jnp.int32, (8, 8), 1)
    four_labels = [
        jnp.sum(jnp.where(entry == column, cls4_ref[t : t + 1, :], 0).astype(F32), axis=1, keepdims=True)
        for t in range(2)
    ]
    unused = jnp.full((8, 110), KINDS, jnp.int32)
    cls_ref[:, :128] = jnp.concatenate([cls5_ref[...], *(x.astype(jnp.int32) for x in four_labels), unused], axis=1)
    cls_ref[:, 128:] = cls6_ref[...]

    def pick(i, carry):
        wanted = jnp.concatenate([src_ref[pl.ds(2 * i, 1), :], src_ref[pl.ds(2 * i + 1, 1), :]], axis=1)
        value = dot(window, onehot(wanted, 256))
        for q in range(2):
            spread(value[:, 128 * q : 128 * q + 128], even, odd, 2 * i + q, slice(128, 256))
        return carry

    lax.fori_loop(0, LIST // 2, pick, 0)

    entries_four = jnp.concatenate([src4_ref[0:1, :], src4_ref[1:2, :]], axis=1)
    wanted = jnp.concatenate(
        [src5_ref[j : j + 1, :] for j in range(LIST)] + [8 * entries_four + o for o in range(8)], axis=1
    )
    wanted = where_held(wanted)
    picked = jnp.zeros((F, 256), F32)
    for k, table in enumerate((t0, t1, t2, t3, t4, t5, t6, t7)):
        picked += dot(table[...], onehot(wanted - 512 * k, 512))
    stack[...] = jnp.zeros(stack.shape, F32)
    for o in range(8):
        stack[o * F : (o + 1) * F, :16] = picked[:, 128 + 16 * o : 144 + 16 * o]
    four = dot(up_ref[...], stack[...].astype(BF)).astype(BF).astype(F32)
    blank = jnp.zeros((F, 110), F32)
    for j in range(LIST):
        value = jnp.concatenate([picked[:, 16 * j : 16 * j + 16], four[:, j : j + 1], four[:, 8 + j : 9 + j], blank], axis=1)
        spread(value, even, odd, j, slice(0, 128))

    def sums(p, carry):
        group([cls_ref[j : j + 1, :] for j in range(LIST)], even, odd, grouped, p)
        return carry

    lax.fori_loop(0, KINDS // 2, sums, 0)
    coarse[...] = dot(maps_ref[...], grouped[...])

    def fill(o, carry):
        row = lax.broadcasted_iota(jnp.int32, (128, 1024), 0)
        cell = lax.broadcasted_iota(jnp.int32, (128, 1024), 1)
        weave[pl.ds(pl.multiple_of(o * 128, 128), 128), :] = jnp.where(cell == 8 * row + o, 1.0, 0.0).astype(BF)
        return carry

    lax.fori_loop(0, 8, fill, 0)
    both[...] = jnp.zeros(both.shape, BF)
    lane = lax.broadcasted_iota(jnp.int32, (F, 128), 1)
    fars[0] = jnp.where(lane < 16, coarse[:, :128], 0.0)
    fars[1] = coarse[:, 128:]
    take = lax.broadcasted_iota(jnp.int32, (128, 128), 0) == lax.broadcasted_iota(jnp.int32, (128, 128), 1) + 16
    local[...] = dot(coarse[:, :128].astype(BF), jnp.where(take, 1.0, 0.0).astype(BF)).astype(BF)

    def woven(lanes):
        pieces = dot(both[...], weave[:, lanes])
        return pieces[:F, :] + pieces[304 : 304 + F, :]

    def fall(level, carry):
        children = dot(down_ref[...], local[...])
        for o in range(8):
            part = children[o * F : (o + 1) * F, :]
            high = part.astype(BF)
            both[:F, 128 * o : 128 * o + 128] = high
            both[304 : 304 + F, 128 * o : 128 * o + 128] = (part - high.astype(F32)).astype(BF)

        @pl.when(level < 2)
        def _():
            local[...] = (woven(slice(0, 128)) + fars[jnp.minimum(level, 1)]).astype(BF)

        return carry

    lax.fori_loop(0, 3, fall, 0)
    for q, seven in enumerate((s0.at[0], s1.at[0], s2.at[0], s2.at[1])):
        lanes = slice(256 * q, 256 * q + 256)
        out_ref[:, lanes] = (woven(lanes) + seven[...]).astype(BF)


def last(tables, six, halo, lists, up, down, sevens, maps):
    return pl.pallas_call(
        last_body,
        out_shape=jax.ShapeDtypeStruct((F, 1024), BF),
        in_specs=[VM] * 22,
        out_specs=VM,
        scratch_shapes=[
            pltpu.VMEM((LIST, F + 8, 256), BF),
            pltpu.VMEM((LIST, F + 8, 256), BF),
            pltpu.VMEM((KINDS * F, 256), BF),
            pltpu.VMEM((8 * F, 128), F32),
            pltpu.VMEM((F, 256), F32),
            pltpu.VMEM((608, 1024), BF),
            pltpu.VMEM((1024, 1024), BF),
            pltpu.VMEM((2, F, 128), F32),
            pltpu.VMEM((F, 128), BF),
            pltpu.VMEM((LIST, 128), jnp.int32),
            pltpu.VMEM((LIST, 256), jnp.int32),
        ],
        compiler_params=pltpu.CompilerParams(vmem_limit_bytes=24 * 2**20),
        cost_estimate=pl.CostEstimate(flops=8 * 10**9, bytes_accessed=12 * 10**6, transcendentals=0),
        name="last",
    )(*tables, six, halo, *lists, up, down, *sevens, maps)


def shifted(value, axis, steps):
    count = lax.axis_size(axis)
    first, last_one = (max(0, -steps), min(count, count - steps))
    return lax.ppermute(value, axis, [(source, source + steps) for source in range(first, last_one)])


def turned(value, axis, size, stride, steps):
    pairs = []
    for source in range(lax.axis_size(axis)):
        position = (source // stride) % size
        target = source + ((position + steps) % size - position) * stride
        pairs.append((source, target))
    return lax.ppermute(value, axis, pairs)


along_z = lambda value, steps: turned(value, "cells", 8, 8, steps)
along_y = lambda value, steps: turned(value, "cells", 4, 2, steps)
along_core = lambda value, steps: turned(value, "cells", 2, 1, steps)
along_x = lambda value, steps: turned(value, "sub", 4, 1, steps)


def tie(*values):
    return lax.optimization_barrier(values)


def body(
    leaf_multipoles,
    occupancy,
    upward_maps,
    transfer_maps,
    downward_maps,
    sources_seven,
    classes_seven,
    sources_six,
    classes_six,
    sources_five,
    classes_five,
    sources_four,
    classes_four,
):
    leaves = leaf_multipoles.T
    up, maps = upward_maps.T, transfer_maps.T
    masked = leaves * occupancy.astype(BF)[None, :]
    lo, hi = masked[:, :512], masked[:, 512:]
    below = shifted(hi, ("cells", "sub"), 1)
    above = shifted(lo, ("cells", "sub"), -1)
    six, five = rise(lo, hi, up)

    src_seven, cls_seven = sources_seven.T, classes_seven.T

    down = flip(downward_maps)
    minus, plus = along_z(five, 1), along_z(five, -1)
    three = jnp.stack([minus, five, plus])
    three, near_lo = tie(three, lo)
    upper = along_z(three, -3)
    lower = along_z(three[1:], 3)
    seven_0 = near(0, 1, below, near_lo, hi, src_seven, cls_seven, maps)
    lower, upper, seven_0 = tie(lower, upper, seven_0)
    column = turn(lower, three, upper)
    column, seven_0, near_lo = tie(column, seven_0, near_lo)
    sides = along_y(column, -1), along_y(column, 2), along_y(column, 1)
    seven_1 = near(1, 1, below, near_lo, hi, src_seven, cls_seven, maps)
    *sides, seven_1 = tie(*sides, seven_1)
    plane = jnp.concatenate([column, *sides], axis=1)
    plane, seven_1, near_lo = tie(plane, seven_1, near_lo)
    tables = [plane, along_x(plane, -1), along_x(plane, 2), along_x(plane, 1)]
    seven_2 = near(2, 2, near_lo, hi, above, src_seven, cls_seven, maps)
    *tables, seven_2, late_up = tie(*tables, seven_2, up)
    tables = tables + [along_core(table, 1) for table in tables]
    halo = halo_six(below, above, late_up)
    sevens = [seven_0, seven_1, seven_2]

    lists = (
        sources_six.T,
        classes_six.T,
        sources_five.T,
        classes_five.T,
        sources_four,
        classes_four,
    )
    return last(tables, six, halo, lists, up, down, sevens, maps).T


def solution(mesh):
    in_specs = (
        P(("cells", "sub"), None),
        P(("cells", "sub")),
        P(),
        P(),
        P(),
        P(("cells", "sub"), None),
        P(("cells", "sub"), None),
        P(("cells", "sub"), None),
        P(("cells", "sub"), None),
        P(("cells", "sub"), None),
        P(("cells", "sub"), None),
        P(("cells", "sub"), None),
        P(("cells", "sub"), None),
    )
    out_specs = P(("cells", "sub"), None)
    return jax.shard_map(body, mesh=mesh, in_specs=in_specs, out_specs=out_specs, check_vma=False)
```

```python
import functools

import jax
import jax.numpy as jnp
from jax import lax
from jax.experimental import pallas as pl
from jax.experimental.pallas import tpu as pltpu
from jax.sharding import PartitionSpec as P

F = 296
KINDS = 32
LIST = 8
BF = jnp.bfloat16
F32 = jnp.float32
VM = pl.BlockSpec(memory_space=pltpu.VMEM)


def place():
    return lax.axis_index("cells") * 4 + lax.axis_index("sub")


def dot(a, b):
    return jnp.dot(a, b, preferred_element_type=F32)


def onehot(rel, depth):
    count = rel.shape[1]
    rows = lax.broadcasted_iota(jnp.int32, (depth, count), 0)
    return jnp.where(rows == rel, 1.0, 0.0).astype(BF)


def split_octants(children, first, width):
    count = children.shape[1]
    source = lax.broadcasted_iota(jnp.int32, (count, 2 * width), 0)
    place = lax.broadcasted_iota(jnp.int32, (count, 2 * width), 1)
    second = (place >= width).astype(jnp.int32)
    wanted = 8 * (place - width * second) + first + second
    return dot(children, jnp.where(source == wanted, 1.0, 0.0).astype(BF))


def ascend(children, up_ref, stack):
    count = children.shape[1]
    source = lax.broadcasted_iota(jnp.int32, (count, 1024), 0)
    column = lax.broadcasted_iota(jnp.int32, (1, 1024), 1)
    both = dot(children, jnp.where(source == 8 * (column & 127) + (column >> 7), 1.0, 0.0).astype(BF))
    for o in range(8):
        stack[o * F : (o + 1) * F, :] = both[:, 128 * o : 128 * o + 128]
    return dot(up_ref[...], stack[...].astype(BF))


def rise_body(lo_ref, hi_ref, up_ref, six_ref, five_ref, stack):
    children = jnp.concatenate([lo_ref[...], hi_ref[...]], axis=1)
    six = ascend(children, up_ref, stack).astype(BF)
    six_ref[...] = six
    source = lax.broadcasted_iota(jnp.int32, (128, 128), 0)
    column = lax.broadcasted_iota(jnp.int32, (1, 128), 1)
    both = dot(six, jnp.where(source == 8 * (column & 15) + (column >> 4), 1.0, 0.0).astype(BF))
    for o in range(8):
        stack[o * F : (o + 1) * F, :16] = both[:, 16 * o : 16 * o + 16]
    five = dot(up_ref[...], stack[...].astype(BF))
    five_ref[...] = five.T[:16, :].astype(BF)


def rise(lo, hi, up):
    return pl.pallas_call(
        rise_body,
        out_shape=(
            jax.ShapeDtypeStruct((F, 128), BF),
            jax.ShapeDtypeStruct((16, F), BF),
        ),
        in_specs=[VM] * 3,
        out_specs=(VM,) * 2,
        scratch_shapes=[pltpu.VMEM((8 * F, 128), F32)],
        compiler_params=pltpu.CompilerParams(vmem_limit_bytes=16 * 2**20),
        cost_estimate=pl.CostEstimate(flops=8 * 10**9, bytes_accessed=3 * 10**6, transcendentals=0),
        name="rise",
    )(lo, hi, up)


def spread(value, even, odd, slot, lanes):
    blank = jnp.zeros((8, value.shape[1]), F32)
    even[slot, :, lanes] = jnp.concatenate([value, blank], axis=0).astype(BF)
    odd[slot, :, lanes] = jnp.concatenate([blank, value], axis=0).astype(BF)


def stack_pair(grouped, row, lanes, even_tile, odd_tile):
    for i in range(18):
        grouped[pl.ds(row + 16 * i, 16), lanes] = even_tile(i)
    grouped[pl.ds(row + 288, 16), lanes] = even_tile(18) + odd_tile(0)
    for i in range(1, 19):
        grouped[pl.ds(row + 288 + 16 * i, 16), lanes] = odd_tile(i)


def group(labels, even, odd, grouped, p):
    wide = [jnp.broadcast_to(label, (16, 256)) for label in labels]

    def masks(kind):
        return [jnp.where(label == kind, 1.0, 0.0).astype(BF) for label in wide]

    first, second = masks(2 * p), masks(2 * p + 1)

    def total(ref, mask, i):
        terms = [ref[j, 16 * i : 16 * i + 16, :] * mask[j] for j in range(LIST)]
        while len(terms) > 1:
            terms = [terms[q] + terms[q + 1] for q in range(0, len(terms), 2)]
        return terms[0]

    stack_pair(
        grouped,
        pl.multiple_of(p * 2 * F, 16),
        slice(None),
        lambda i: total(even, first, i),
        lambda i: total(odd, second, i),
    )


def near_body(block, count, a_ref, b_ref, c_ref, src_ref, cls_ref, maps_ref, out_ref, window, even, odd, grouped):
    side = block % 2
    for k in range(4 + count):
        half = k + side
        window[:, 256 * k : 256 * k + 256] = (a_ref, b_ref, c_ref)[half // 2][:, 256 * (half % 2) : 256 * (half % 2) + 256]

    def pick(i, carry):
        local, four = i // 2, i % 2
        base = pl.multiple_of(local * 256, 256)
        lanes = pl.ds(pl.multiple_of((block + local) * 256, 256), 256)
        start = place() * 1024 - 512 + (block + local) * 256
        wanted = [onehot(src_ref[pl.ds(4 * four + q, 1), lanes] - start, 1280) for q in range(4)]
        value = dot(window[:, pl.ds(base, 1280)], jnp.concatenate(wanted, axis=1))
        for q in range(4):
            spread(value[:, 256 * q : 256 * q + 256], even.at[local], odd.at[local], 4 * four + q, slice(None))
        return carry

    lax.fori_loop(0, 2 * count, pick, 0)

    def sums(i, carry):
        local, p = i // 16, i % 16
        lanes = pl.ds(pl.multiple_of((block + local) * 256, 256), 256)
        labels = [cls_ref[j : j + 1, lanes] for j in range(LIST)]
        group(labels, even.at[local], odd.at[local], grouped.at[local], p)
        return carry

    lax.fori_loop(0, 16 * count, sums, 0)

    def send(i, carry):
        out_ref[i] = dot(maps_ref[...], grouped[i])
        return carry

    lax.fori_loop(0, count, send, 0)


def near(block, count, a, b, c, src, cls, maps):
    return pl.pallas_call(
        functools.partial(near_body, block, count),
        out_shape=jax.ShapeDtypeStruct((count, F, 256), F32),
        in_specs=[VM] * 6,
        out_specs=VM,
        scratch_shapes=[
            pltpu.VMEM((F, 1024 + 256 * count), BF),
            pltpu.VMEM((count, LIST, F + 8, 256), BF),
            pltpu.VMEM((count, LIST, F + 8, 256), BF),
            pltpu.VMEM((count, KINDS * F, 256), BF),
        ],
        compiler_params=pltpu.CompilerParams(vmem_limit_bytes=(22 if count > 1 else 16) * 2**20),
        cost_estimate=pl.CostEstimate(flops=count * 6 * 10**9, bytes_accessed=6 * 10**6, transcendentals=0),
        name=f"near{block}",
    )(a, b, c, src, cls, maps)


def turn_body(lower_ref, middle_ref, upper_ref, out_ref):
    parts = [ref[k].astype(F32) for ref in (lower_ref, middle_ref, upper_ref) for k in range(ref.shape[0])]
    out_ref[...] = jnp.concatenate(parts, axis=0).T.astype(BF)


def turn(lower, three, upper):
    return pl.pallas_call(
        turn_body,
        out_shape=jax.ShapeDtypeStruct((F, 128), BF),
        in_specs=[VM] * 3,
        out_specs=VM,
        compiler_params=pltpu.CompilerParams(vmem_limit_bytes=8 * 2**20),
        cost_estimate=pl.CostEstimate(flops=10**8, bytes_accessed=10**5, transcendentals=0),
        name="turn",
    )(lower, three, upper)


def halo_body(below_ref, above_ref, up_ref, out_ref, stack):
    children = jnp.concatenate([below_ref[...], above_ref[...]], axis=1)
    out_ref[...] = ascend(children, up_ref, stack).astype(BF)


def halo_six(below, above, up):
    return pl.pallas_call(
        halo_body,
        out_shape=jax.ShapeDtypeStruct((F, 128), BF),
        in_specs=[VM] * 3,
        out_specs=VM,
        scratch_shapes=[pltpu.VMEM((8 * F, 128), F32)],
        compiler_params=pltpu.CompilerParams(vmem_limit_bytes=16 * 2**20),
        cost_estimate=pl.CostEstimate(flops=2 * 10**9, bytes_accessed=3 * 10**6, transcendentals=0),
        name="halo",
    )(below, above, up)


def flip_body(down_ref, out_ref):
    out_ref[...] = down_ref[...].T


def flip(down):
    return pl.pallas_call(
        flip_body,
        out_shape=jax.ShapeDtypeStruct((8 * F, F), BF),
        in_specs=[VM],
        out_specs=VM,
        compiler_params=pltpu.CompilerParams(vmem_limit_bytes=16 * 2**20),
        cost_estimate=pl.CostEstimate(flops=10**9, bytes_accessed=3 * 10**6, transcendentals=0),
        name="flip",
    )(down)


def where_held(cell):
    cells, sub = lax.axis_index("cells"), lax.axis_index("sub")
    there = cell >> 6
    dz = ((there >> 3) - (cells >> 3) + 3) & 7
    dy = ((there >> 1) - (cells >> 1)) & 3
    dc = (there - cells) & 1
    dx = ((cell >> 4) - sub) & 3
    return (dc * 4 + dx) * 512 + dy * 128 + dz * 16 + (cell & 15)


def last_body(
    t0, t1, t2, t3, t4, t5, t6, t7, six_ref, halo_ref, src6_ref, cls6_ref, src5_ref, cls5_ref, src4_ref, cls4_ref,
    up_ref, down_ref,
    s0, s1, s2, maps_ref, out_ref,
    even, odd, grouped, stack, coarse, octants, weave, fars, local, src_ref, cls_ref,
):
    window = jnp.concatenate([six_ref[...], halo_ref[...]], axis=1)
    rel = src6_ref[...] - (place() * 128 - 64)
    src_ref[...] = jnp.where(rel < 64, rel + 128, jnp.where(rel < 192, rel - 64, rel))
    entry = lax.broadcasted_iota(jnp.int32, (8, 8), 0)
    column = lax.broadcasted_iota(jnp.int32, (8, 8), 1)
    four_labels = [
        jnp.sum(jnp.where(entry == column, cls4_ref[t : t + 1, :], 0).astype(F32), axis=1, keepdims=True)
        for t in range(2)
    ]
    unused = jnp.full((8, 110), KINDS, jnp.int32)
    cls_ref[:, :128] = jnp.concatenate([cls5_ref[...], *(x.astype(jnp.int32) for x in four_labels), unused], axis=1)
    cls_ref[:, 128:] = cls6_ref[...]

    def pick(i, carry):
        wanted = jnp.concatenate([src_ref[pl.ds(2 * i, 1), :], src_ref[pl.ds(2 * i + 1, 1), :]], axis=1)
        value = dot(window, onehot(wanted, 256))
        for q in range(2):
            spread(value[:, 128 * q : 128 * q + 128], even, odd, 2 * i + q, slice(128, 256))
        return carry

    lax.fori_loop(0, LIST // 2, pick, 0)

    entries_four = jnp.concatenate([src4_ref[0:1, :], src4_ref[1:2, :]], axis=1)
    wanted = jnp.concatenate(
        [src5_ref[j : j + 1, :] for j in range(LIST)] + [8 * entries_four + o for o in range(8)], axis=1
    )
    wanted = where_held(wanted)
    picked = jnp.zeros((F, 256), F32)
    for k, table in enumerate((t0, t1, t2, t3, t4, t5, t6, t7)):
        picked += dot(table[...], onehot(wanted - 512 * k, 512))
    stack[...] = jnp.zeros(stack.shape, F32)
    for o in range(8):
        stack[o * F : (o + 1) * F, :16] = picked[:, 128 + 16 * o : 144 + 16 * o]
    four = dot(up_ref[...], stack[...].astype(BF)).astype(BF).astype(F32)
    blank = jnp.zeros((F, 110), F32)
    for j in range(LIST):
        value = jnp.concatenate([picked[:, 16 * j : 16 * j + 16], four[:, j : j + 1], four[:, 8 + j : 9 + j], blank], axis=1)
        spread(value, even, odd, j, slice(0, 128))

    def sums(p, carry):
        group([cls_ref[j : j + 1, :] for j in range(LIST)], even, odd, grouped, p)
        return carry

    lax.fori_loop(0, KINDS // 2, sums, 0)
    coarse[...] = dot(maps_ref[...], grouped[...])

    def fill(o, carry):
        row = lax.broadcasted_iota(jnp.int32, (128, 1024), 0)
        cell = lax.broadcasted_iota(jnp.int32, (128, 1024), 1)
        weave[pl.ds(pl.multiple_of(o * 128, 128), 128), :] = jnp.where(cell == 8 * row + o, 1.0, 0.0).astype(BF)
        return carry

    lax.fori_loop(0, 8, fill, 0)
    lane = lax.broadcasted_iota(jnp.int32, (F, 128), 1)
    fars[0] = jnp.where(lane < 16, coarse[:, :128], 0.0)
    fars[1] = coarse[:, 128:]
    take = lax.broadcasted_iota(jnp.int32, (128, 128), 0) == lax.broadcasted_iota(jnp.int32, (128, 128), 1) + 16
    local[...] = dot(coarse[:, :128].astype(BF), jnp.where(take, 1.0, 0.0).astype(BF)).astype(BF)

    def woven(lanes):
        return dot(octants[...], weave[:, lanes])

    def fall(level, carry):
        children = dot(down_ref[...], local[...])
        for o in range(8):
            octants[:, 128 * o : 128 * o + 128] = children[o * F : (o + 1) * F, :].astype(BF)

        @pl.when(level < 2)
        def _():
            local[...] = (woven(slice(0, 128)) + fars[jnp.minimum(level, 1)]).astype(BF)

        return carry

    lax.fori_loop(0, 3, fall, 0)
    for q, seven in enumerate((s0.at[0], s1.at[0], s2.at[0], s2.at[1])):
        lanes = slice(256 * q, 256 * q + 256)
        out_ref[:, lanes] = (woven(lanes) + seven[...]).astype(BF)


def last(tables, six, halo, lists, up, down, sevens, maps):
    return pl.pallas_call(
        last_body,
        out_shape=jax.ShapeDtypeStruct((F, 1024), BF),
        in_specs=[VM] * 22,
        out_specs=VM,
        scratch_shapes=[
            pltpu.VMEM((LIST, F + 8, 256), BF),
            pltpu.VMEM((LIST, F + 8, 256), BF),
            pltpu.VMEM((KINDS * F, 256), BF),
            pltpu.VMEM((8 * F, 128), F32),
            pltpu.VMEM((F, 256), F32),
            pltpu.VMEM((F, 1024), BF),
            pltpu.VMEM((1024, 1024), BF),
            pltpu.VMEM((2, F, 128), F32),
            pltpu.VMEM((F, 128), BF),
            pltpu.VMEM((LIST, 128), jnp.int32),
            pltpu.VMEM((LIST, 256), jnp.int32),
        ],
        compiler_params=pltpu.CompilerParams(vmem_limit_bytes=24 * 2**20),
        cost_estimate=pl.CostEstimate(flops=8 * 10**9, bytes_accessed=12 * 10**6, transcendentals=0),
        name="last",
    )(*tables, six, halo, *lists, up, down, *sevens, maps)


def shifted(value, axis, steps):
    count = lax.axis_size(axis)
    first, last_one = (max(0, -steps), min(count, count - steps))
    return lax.ppermute(value, axis, [(source, source + steps) for source in range(first, last_one)])


def turned(value, axis, size, stride, steps):
    pairs = []
    for source in range(lax.axis_size(axis)):
        position = (source // stride) % size
        target = source + ((position + steps) % size - position) * stride
        pairs.append((source, target))
    return lax.ppermute(value, axis, pairs)


along_z = lambda value, steps: turned(value, "cells", 8, 8, steps)
along_y = lambda value, steps: turned(value, "cells", 4, 2, steps)
along_core = lambda value, steps: turned(value, "cells", 2, 1, steps)
along_x = lambda value, steps: turned(value, "sub", 4, 1, steps)


def tie(*values):
    return lax.optimization_barrier(values)


def body(
    leaf_multipoles,
    occupancy,
    upward_maps,
    transfer_maps,
    downward_maps,
    sources_seven,
    classes_seven,
    sources_six,
    classes_six,
    sources_five,
    classes_five,
    sources_four,
    classes_four,
):
    leaves = leaf_multipoles.T
    up, maps = upward_maps.T, transfer_maps.T
    masked = leaves * occupancy.astype(BF)[None, :]
    lo, hi = masked[:, :512], masked[:, 512:]
    below = shifted(hi, ("cells", "sub"), 1)
    above = shifted(lo, ("cells", "sub"), -1)
    six, five = rise(lo, hi, up)

    src_seven, cls_seven = sources_seven.T, classes_seven.T

    down = flip(downward_maps)
    minus, plus = along_z(five, 1), along_z(five, -1)
    three = jnp.stack([minus, five, plus])
    three, near_lo = tie(three, lo)
    upper = along_z(three, -3)
    lower = along_z(three[1:], 3)
    seven_0 = near(0, 1, below, near_lo, hi, src_seven, cls_seven, maps)
    lower, upper, seven_0 = tie(lower, upper, seven_0)
    column = turn(lower, three, upper)
    column, seven_0, near_lo = tie(column, seven_0, near_lo)
    sides = along_y(column, -1), along_y(column, 2), along_y(column, 1)
    seven_1 = near(1, 1, below, near_lo, hi, src_seven, cls_seven, maps)
    *sides, seven_1 = tie(*sides, seven_1)
    plane = jnp.concatenate([column, *sides], axis=1)
    plane, seven_1, near_lo = tie(plane, seven_1, near_lo)
    tables = [plane, along_x(plane, -1), along_x(plane, 2), along_x(plane, 1)]
    seven_2 = near(2, 2, near_lo, hi, above, src_seven, cls_seven, maps)
    *tables, seven_2, late_up = tie(*tables, seven_2, up)
    tables = tables + [along_core(table, 1) for table in tables]
    halo = halo_six(below, above, late_up)
    sevens = [seven_0, seven_1, seven_2]

    lists = (
        sources_six.T,
        classes_six.T,
        sources_five.T,
        classes_five.T,
        sources_four,
        classes_four,
    )
    return last(tables, six, halo, lists, up, down, sevens, maps).T


def solution(mesh):
    in_specs = (
        P(("cells", "sub"), None),
        P(("cells", "sub")),
        P(),
        P(),
        P(),
        P(("cells", "sub"), None),
        P(("cells", "sub"), None),
        P(("cells", "sub"), None),
        P(("cells", "sub"), None),
        P(("cells", "sub"), None),
        P(("cells", "sub"), None),
        P(("cells", "sub"), None),
        P(("cells", "sub"), None),
    )
    out_specs = P(("cells", "sub"), None)
    return jax.shard_map(body, mesh=mesh, in_specs=in_specs, out_specs=out_specs, check_vma=False)
```

```python
import functools

import jax
import jax.numpy as jnp
from jax import lax
from jax.experimental import pallas as pl
from jax.experimental.pallas import tpu as pltpu
from jax.sharding import PartitionSpec as P

F = 296
KINDS = 32
LIST = 8
BF = jnp.bfloat16
F32 = jnp.float32
VM = pl.BlockSpec(memory_space=pltpu.VMEM)


def place():
    return lax.axis_index("cells") * 4 + lax.axis_index("sub")


def dot(a, b):
    return jnp.dot(a, b, preferred_element_type=F32)


def onehot(rel, depth):
    count = rel.shape[1]
    rows = lax.broadcasted_iota(jnp.int32, (depth, count), 0)
    return jnp.where(rows == rel, 1.0, 0.0).astype(BF)


def split_octants(children, first, width):
    count = children.shape[1]
    source = lax.broadcasted_iota(jnp.int32, (count, 2 * width), 0)
    place = lax.broadcasted_iota(jnp.int32, (count, 2 * width), 1)
    second = (place >= width).astype(jnp.int32)
    wanted = 8 * (place - width * second) + first + second
    return dot(children, jnp.where(source == wanted, 1.0, 0.0).astype(BF))


def ascend(children, up_ref, stack):
    count = children.shape[1]
    source = lax.broadcasted_iota(jnp.int32, (count, 1024), 0)
    column = lax.broadcasted_iota(jnp.int32, (1, 1024), 1)
    both = dot(children, jnp.where(source == 8 * (column & 127) + (column >> 7), 1.0, 0.0).astype(BF))
    for o in range(8):
        stack[o * F : (o + 1) * F, :] = both[:, 128 * o : 128 * o + 128]
    return dot(up_ref[...], stack[...].astype(BF))


def rise_body(lo_ref, hi_ref, up_ref, six_ref, five_ref, stack):
    children = jnp.concatenate([lo_ref[...], hi_ref[...]], axis=1)
    six = ascend(children, up_ref, stack).astype(BF)
    six_ref[...] = six
    source = lax.broadcasted_iota(jnp.int32, (128, 128), 0)
    column = lax.broadcasted_iota(jnp.int32, (1, 128), 1)
    both = dot(six, jnp.where(source == 8 * (column & 15) + (column >> 4), 1.0, 0.0).astype(BF))
    for o in range(8):
        stack[o * F : (o + 1) * F, :16] = both[:, 16 * o : 16 * o + 16]
    five = dot(up_ref[...], stack[...].astype(BF))
    five_ref[...] = five.T[:16, :].astype(BF)


def rise(lo, hi, up):
    return pl.pallas_call(
        rise_body,
        out_shape=(
            jax.ShapeDtypeStruct((F, 128), BF),
            jax.ShapeDtypeStruct((16, F), BF),
        ),
        in_specs=[VM] * 3,
        out_specs=(VM,) * 2,
        scratch_shapes=[pltpu.VMEM((8 * F, 128), F32)],
        compiler_params=pltpu.CompilerParams(vmem_limit_bytes=16 * 2**20),
        cost_estimate=pl.CostEstimate(flops=8 * 10**9, bytes_accessed=3 * 10**6, transcendentals=0),
        name="rise",
    )(lo, hi, up)


def spread(value, even, odd, slot, lanes):
    blank = jnp.zeros((8, value.shape[1]), F32)
    even[slot, :, lanes] = jnp.concatenate([value, blank], axis=0).astype(BF)
    odd[slot, :, lanes] = jnp.concatenate([blank, value], axis=0).astype(BF)


def stack_pair(grouped, row, lanes, even_tile, odd_tile):
    for i in range(18):
        grouped[pl.ds(row + 16 * i, 16), lanes] = even_tile(i)
    grouped[pl.ds(row + 288, 16), lanes] = even_tile(18) + odd_tile(0)
    for i in range(1, 19):
        grouped[pl.ds(row + 288 + 16 * i, 16), lanes] = odd_tile(i)


def group(labels, even, odd, grouped, p):
    wide = [jnp.broadcast_to(label, (16, 256)) for label in labels]

    def masks(kind):
        return [jnp.where(label == kind, 1.0, 0.0).astype(BF) for label in wide]

    first, second = masks(2 * p), masks(2 * p + 1)

    def total(ref, mask, i):
        terms = [ref[j, 16 * i : 16 * i + 16, :] * mask[j] for j in range(LIST)]
        while len(terms) > 1:
            terms = [terms[q] + terms[q + 1] for q in range(0, len(terms), 2)]
        return terms[0]

    stack_pair(
        grouped,
        pl.multiple_of(p * 2 * F, 16),
        slice(None),
        lambda i: total(even, first, i),
        lambda i: total(odd, second, i),
    )


def near_body(block, count, a_ref, b_ref, c_ref, src_ref, cls_ref, maps_ref, out_ref, window, even, odd, grouped):
    side = block % 2
    for k in range(4 + count):
        half = k + side
        window[:, 256 * k : 256 * k + 256] = (a_ref, b_ref, c_ref)[half // 2][:, 256 * (half % 2) : 256 * (half % 2) + 256]

    def pick(i, carry):
        local, four = i // 2, i % 2
        base = pl.multiple_of(local * 256, 256)
        lanes = pl.ds(pl.multiple_of((block + local) * 256, 256), 256)
        start = place() * 1024 - 512 + (block + local) * 256
        wanted = [onehot(src_ref[pl.ds(4 * four + q, 1), lanes] - start, 1280) for q in range(4)]
        value = dot(window[:, pl.ds(base, 1280)], jnp.concatenate(wanted, axis=1))
        for q in range(4):
            spread(value[:, 256 * q : 256 * q + 256], even.at[local], odd.at[local], 4 * four + q, slice(None))
        return carry

    lax.fori_loop(0, 2 * count, pick, 0)

    def sums(i, carry):
        local, p = i // 16, i % 16
        lanes = pl.ds(pl.multiple_of((block + local) * 256, 256), 256)
        labels = [cls_ref[j : j + 1, lanes] for j in range(LIST)]
        group(labels, even.at[local], odd.at[local], grouped.at[local], p)
        return carry

    lax.fori_loop(0, 16 * count, sums, 0)

    def send(i, carry):
        out_ref[i] = dot(maps_ref[...], grouped[i])
        return carry

    lax.fori_loop(0, count, send, 0)


def near(block, count, a, b, c, src, cls, maps):
    return pl.pallas_call(
        functools.partial(near_body, block, count),
        out_shape=jax.ShapeDtypeStruct((count, F, 256), F32),
        in_specs=[VM] * 6,
        out_specs=VM,
        scratch_shapes=[
            pltpu.VMEM((F, 1024 + 256 * count), BF),
            pltpu.VMEM((count, LIST, F + 8, 256), BF),
            pltpu.VMEM((count, LIST, F + 8, 256), BF),
            pltpu.VMEM((count, KINDS * F, 256), BF),
        ],
        compiler_params=pltpu.CompilerParams(vmem_limit_bytes=(22 if count > 1 else 16) * 2**20),
        cost_estimate=pl.CostEstimate(flops=count * 6 * 10**9, bytes_accessed=6 * 10**6, transcendentals=0),
        name=f"near{block}",
    )(a, b, c, src, cls, maps)


def turn_body(even_ref, odd_ref, out_ref):
    parts = [ref[k].astype(F32) for ref in (even_ref, odd_ref) for k in range(4)]
    out_ref[...] = jnp.concatenate(parts, axis=0).T.astype(BF)


def turn(fours, between):
    return pl.pallas_call(
        turn_body,
        out_shape=jax.ShapeDtypeStruct((F, 128), BF),
        in_specs=[VM] * 2,
        out_specs=VM,
        compiler_params=pltpu.CompilerParams(vmem_limit_bytes=8 * 2**20),
        cost_estimate=pl.CostEstimate(flops=10**8, bytes_accessed=10**5, transcendentals=0),
        name="turn",
    )(fours, between)


def halo_body(below_ref, above_ref, up_ref, out_ref, stack):
    children = jnp.concatenate([below_ref[...], above_ref[...]], axis=1)
    out_ref[...] = ascend(children, up_ref, stack).astype(BF)


def halo_six(below, above, up):
    return pl.pallas_call(
        halo_body,
        out_shape=jax.ShapeDtypeStruct((F, 128), BF),
        in_specs=[VM] * 3,
        out_specs=VM,
        scratch_shapes=[pltpu.VMEM((8 * F, 128), F32)],
        compiler_params=pltpu.CompilerParams(vmem_limit_bytes=16 * 2**20),
        cost_estimate=pl.CostEstimate(flops=2 * 10**9, bytes_accessed=3 * 10**6, transcendentals=0),
        name="halo",
    )(below, above, up)


def flip_body(down_ref, out_ref):
    out_ref[...] = down_ref[...].T


def flip(down):
    return pl.pallas_call(
        flip_body,
        out_shape=jax.ShapeDtypeStruct((8 * F, F), BF),
        in_specs=[VM],
        out_specs=VM,
        compiler_params=pltpu.CompilerParams(vmem_limit_bytes=16 * 2**20),
        cost_estimate=pl.CostEstimate(flops=10**9, bytes_accessed=3 * 10**6, transcendentals=0),
        name="flip",
    )(down)


def where_held(cell):
    cells, sub = lax.axis_index("cells"), lax.axis_index("sub")
    there = cell >> 6
    dz = ((there >> 3) - (cells >> 3)) & 7
    dy = ((there >> 1) - (cells >> 1)) & 3
    dc = (there - cells) & 1
    dx = ((cell >> 4) - sub) & 3
    return (dc * 4 + dx) * 512 + dy * 128 + ((dz >> 1) + 4 * (dz & 1)) * 16 + (cell & 15)


def last_body(
    t0, t1, t2, t3, t4, t5, t6, t7, six_ref, halo_ref, src6_ref, cls6_ref, src5_ref, cls5_ref, src4_ref, cls4_ref,
    up_ref, down_ref,
    s0, s1, s2, maps_ref, out_ref,
    even, odd, grouped, stack, coarse, octants, weave, fars, local, src_ref, cls_ref,
):
    window = jnp.concatenate([six_ref[...], halo_ref[...]], axis=1)
    rel = src6_ref[...] - (place() * 128 - 64)
    src_ref[...] = jnp.where(rel < 64, rel + 128, jnp.where(rel < 192, rel - 64, rel))
    entry = lax.broadcasted_iota(jnp.int32, (8, 8), 0)
    column = lax.broadcasted_iota(jnp.int32, (8, 8), 1)
    four_labels = [
        jnp.sum(jnp.where(entry == column, cls4_ref[t : t + 1, :], 0).astype(F32), axis=1, keepdims=True)
        for t in range(2)
    ]
    unused = jnp.full((8, 110), KINDS, jnp.int32)
    cls_ref[:, :128] = jnp.concatenate([cls5_ref[...], *(x.astype(jnp.int32) for x in four_labels), unused], axis=1)
    cls_ref[:, 128:] = cls6_ref[...]

    def pick(i, carry):
        wanted = jnp.concatenate([src_ref[pl.ds(2 * i, 1), :], src_ref[pl.ds(2 * i + 1, 1), :]], axis=1)
        value = dot(window, onehot(wanted, 256))
        for q in range(2):
            spread(value[:, 128 * q : 128 * q + 128], even, odd, 2 * i + q, slice(128, 256))
        return carry

    lax.fori_loop(0, LIST // 2, pick, 0)

    entries_four = jnp.concatenate([src4_ref[0:1, :], src4_ref[1:2, :]], axis=1)
    wanted = jnp.concatenate(
        [src5_ref[j : j + 1, :] for j in range(LIST)] + [8 * entries_four + o for o in range(8)], axis=1
    )
    wanted = where_held(wanted)
    picked = jnp.zeros((F, 256), F32)
    for k, table in enumerate((t0, t1, t2, t3, t4, t5, t6, t7)):
        picked += dot(table[...], onehot(wanted - 512 * k, 512))
    stack[...] = jnp.zeros(stack.shape, F32)
    for o in range(8):
        stack[o * F : (o + 1) * F, :16] = picked[:, 128 + 16 * o : 144 + 16 * o]
    four = dot(up_ref[...], stack[...].astype(BF)).astype(BF).astype(F32)
    blank = jnp.zeros((F, 110), F32)
    for j in range(LIST):
        value = jnp.concatenate([picked[:, 16 * j : 16 * j + 16], four[:, j : j + 1], four[:, 8 + j : 9 + j], blank], axis=1)
        spread(value, even, odd, j, slice(0, 128))

    def sums(p, carry):
        group([cls_ref[j : j + 1, :] for j in range(LIST)], even, odd, grouped, p)
        return carry

    lax.fori_loop(0, KINDS // 2, sums, 0)
    coarse[...] = dot(maps_ref[...], grouped[...])

    def fill(o, carry):
        row = lax.broadcasted_iota(jnp.int32, (128, 1024), 0)
        cell = lax.broadcasted_iota(jnp.int32, (128, 1024), 1)
        weave[pl.ds(pl.multiple_of(o * 128, 128), 128), :] = jnp.where(cell == 8 * row + o, 1.0, 0.0).astype(BF)
        return carry

    lax.fori_loop(0, 8, fill, 0)
    lane = lax.broadcasted_iota(jnp.int32, (F, 128), 1)
    fars[0] = jnp.where(lane < 16, coarse[:, :128], 0.0)
    fars[1] = coarse[:, 128:]
    take = lax.broadcasted_iota(jnp.int32, (128, 128), 0) == lax.broadcasted_iota(jnp.int32, (128, 128), 1) + 16
    local[...] = dot(coarse[:, :128].astype(BF), jnp.where(take, 1.0, 0.0).astype(BF)).astype(BF)

    def woven(lanes):
        return dot(octants[...], weave[:, lanes])

    def fall(level, carry):
        children = dot(down_ref[...], local[...])
        for o in range(8):
            octants[:, 128 * o : 128 * o + 128] = children[o * F : (o + 1) * F, :].astype(BF)

        @pl.when(level < 2)
        def _():
            local[...] = (woven(slice(0, 128)) + fars[jnp.minimum(level, 1)]).astype(BF)

        return carry

    lax.fori_loop(0, 3, fall, 0)
    for q, seven in enumerate((s0.at[0], s1.at[0], s2.at[0], s2.at[1])):
        lanes = slice(256 * q, 256 * q + 256)
        out_ref[:, lanes] = (woven(lanes) + seven[...]).astype(BF)


def last(tables, six, halo, lists, up, down, sevens, maps):
    return pl.pallas_call(
        last_body,
        out_shape=jax.ShapeDtypeStruct((F, 1024), BF),
        in_specs=[VM] * 22,
        out_specs=VM,
        scratch_shapes=[
            pltpu.VMEM((LIST, F + 8, 256), BF),
            pltpu.VMEM((LIST, F + 8, 256), BF),
            pltpu.VMEM((KINDS * F, 256), BF),
            pltpu.VMEM((8 * F, 128), F32),
            pltpu.VMEM((F, 256), F32),
            pltpu.VMEM((F, 1024), BF),
            pltpu.VMEM((1024, 1024), BF),
            pltpu.VMEM((2, F, 128), F32),
            pltpu.VMEM((F, 128), BF),
            pltpu.VMEM((LIST, 128), jnp.int32),
            pltpu.VMEM((LIST, 256), jnp.int32),
        ],
        compiler_params=pltpu.CompilerParams(vmem_limit_bytes=24 * 2**20),
        cost_estimate=pl.CostEstimate(flops=8 * 10**9, bytes_accessed=12 * 10**6, transcendentals=0),
        name="last",
    )(*tables, six, halo, *lists, up, down, *sevens, maps)


def shifted(value, axis, steps):
    count = lax.axis_size(axis)
    first, last_one = (max(0, -steps), min(count, count - steps))
    return lax.ppermute(value, axis, [(source, source + steps) for source in range(first, last_one)])


def turned(value, axis, size, stride, steps):
    pairs = []
    for source in range(lax.axis_size(axis)):
        position = (source // stride) % size
        target = source + ((position + steps) % size - position) * stride
        pairs.append((source, target))
    return lax.ppermute(value, axis, pairs)


along_z = lambda value, steps: turned(value, "cells", 8, 8, steps)
along_y = lambda value, steps: turned(value, "cells", 4, 2, steps)
along_core = lambda value, steps: turned(value, "cells", 2, 1, steps)
along_x = lambda value, steps: turned(value, "sub", 4, 1, steps)


def tie(*values):
    return lax.optimization_barrier(values)


def body(
    leaf_multipoles,
    occupancy,
    upward_maps,
    transfer_maps,
    downward_maps,
    sources_seven,
    classes_seven,
    sources_six,
    classes_six,
    sources_five,
    classes_five,
    sources_four,
    classes_four,
):
    leaves = leaf_multipoles.T
    up, maps = upward_maps.T, transfer_maps.T
    masked = leaves * occupancy.astype(BF)[None, :]
    lo, hi = masked[:, :512], masked[:, 512:]
    below = shifted(hi, ("cells", "sub"), 1)
    above = shifted(lo, ("cells", "sub"), -1)
    six, five = rise(lo, hi, up)

    src_seven, cls_seven = sources_seven.T, classes_seven.T

    down = flip(downward_maps)
    fours = jnp.stack([five, along_z(five, -2), along_z(five, 4), along_z(five, 2)])
    fours, near_lo = tie(fours, lo)
    between = along_z(fours, -1)
    seven_0 = near(0, 1, below, near_lo, hi, src_seven, cls_seven, maps)
    between, seven_0 = tie(between, seven_0)
    column = turn(fours, between)
    column, seven_0, near_lo = tie(column, seven_0, near_lo)
    sides = along_y(column, -1), along_y(column, 2), along_y(column, 1)
    seven_1 = near(1, 1, below, near_lo, hi, src_seven, cls_seven, maps)
    *sides, seven_1 = tie(*sides, seven_1)
    plane = jnp.concatenate([column, *sides], axis=1)
    plane, seven_1, near_lo = tie(plane, seven_1, near_lo)
    tables = [plane, along_x(plane, -1), along_x(plane, 2), along_x(plane, 1)]
    seven_2 = near(2, 2, near_lo, hi, above, src_seven, cls_seven, maps)
    *tables, seven_2, late_up = tie(*tables, seven_2, up)
    tables = tables + [along_core(table, 1) for table in tables]
    halo = halo_six(below, above, late_up)
    sevens = [seven_0, seven_1, seven_2]

    lists = (
        sources_six.T,
        classes_six.T,
        sources_five.T,
        classes_five.T,
        sources_four,
        classes_four,
    )
    return last(tables, six, halo, lists, up, down, sevens, maps).T


def solution(mesh):
    in_specs = (
        P(("cells", "sub"), None),
        P(("cells", "sub")),
        P(),
        P(),
        P(),
        P(("cells", "sub"), None),
        P(("cells", "sub"), None),
        P(("cells", "sub"), None),
        P(("cells", "sub"), None),
        P(("cells", "sub"), None),
        P(("cells", "sub"), None),
        P(("cells", "sub"), None),
        P(("cells", "sub"), None),
    )
    out_specs = P(("cells", "sub"), None)
    return jax.shard_map(body, mesh=mesh, in_specs=in_specs, out_specs=out_specs, check_vma=False)
```

```python
import functools

import jax
import jax.numpy as jnp
from jax import lax
from jax.experimental import pallas as pl
from jax.experimental.pallas import tpu as pltpu
from jax.sharding import PartitionSpec as P

F = 296
KINDS = 32
LIST = 8
BF = jnp.bfloat16
F32 = jnp.float32
VM = pl.BlockSpec(memory_space=pltpu.VMEM)


def place():
    return lax.axis_index("cells") * 4 + lax.axis_index("sub")


def dot(a, b):
    return jnp.dot(a, b, preferred_element_type=F32)


def onehot(rel, depth):
    count = rel.shape[1]
    rows = lax.broadcasted_iota(jnp.int32, (depth, count), 0)
    return jnp.where(rows == rel, 1.0, 0.0).astype(BF)


def split_octants(children, first, width):
    count = children.shape[1]
    source = lax.broadcasted_iota(jnp.int32, (count, 2 * width), 0)
    place = lax.broadcasted_iota(jnp.int32, (count, 2 * width), 1)
    second = (place >= width).astype(jnp.int32)
    wanted = 8 * (place - width * second) + first + second
    return dot(children, jnp.where(source == wanted, 1.0, 0.0).astype(BF))


def ascend(children, up_ref, stack):
    count = children.shape[1]
    source = lax.broadcasted_iota(jnp.int32, (count, 1024), 0)
    column = lax.broadcasted_iota(jnp.int32, (1, 1024), 1)
    both = dot(children, jnp.where(source == 8 * (column & 127) + (column >> 7), 1.0, 0.0).astype(BF))
    for o in range(8):
        stack[o * F : (o + 1) * F, :] = both[:, 128 * o : 128 * o + 128]
    return dot(up_ref[...], stack[...].astype(BF))


def rise_body(lo_ref, hi_ref, up_ref, six_ref, five_ref, stack):
    children = jnp.concatenate([lo_ref[...], hi_ref[...]], axis=1)
    six = ascend(children, up_ref, stack).astype(BF)
    six_ref[...] = six
    source = lax.broadcasted_iota(jnp.int32, (128, 128), 0)
    column = lax.broadcasted_iota(jnp.int32, (1, 128), 1)
    both = dot(six, jnp.where(source == 8 * (column & 15) + (column >> 4), 1.0, 0.0).astype(BF))
    for o in range(8):
        stack[o * F : (o + 1) * F, :16] = both[:, 16 * o : 16 * o + 16]
    five = dot(up_ref[...], stack[...].astype(BF))
    five_ref[...] = five.T[:16, :].astype(BF)


def rise(lo, hi, up):
    return pl.pallas_call(
        rise_body,
        out_shape=(
            jax.ShapeDtypeStruct((F, 128), BF),
            jax.ShapeDtypeStruct((16, F), BF),
        ),
        in_specs=[VM] * 3,
        out_specs=(VM,) * 2,
        scratch_shapes=[pltpu.VMEM((8 * F, 128), F32)],
        compiler_params=pltpu.CompilerParams(vmem_limit_bytes=16 * 2**20),
        cost_estimate=pl.CostEstimate(flops=8 * 10**9, bytes_accessed=3 * 10**6, transcendentals=0),
        name="rise",
    )(lo, hi, up)


def spread(value, even, odd, slot, lanes):
    blank = jnp.zeros((8, value.shape[1]), F32)
    even[slot, :, lanes] = jnp.concatenate([value, blank], axis=0).astype(BF)
    odd[slot, :, lanes] = jnp.concatenate([blank, value], axis=0).astype(BF)


def stack_pair(grouped, row, lanes, even_tile, odd_tile):
    for i in range(18):
        grouped[pl.ds(row + 16 * i, 16), lanes] = even_tile(i)
    grouped[pl.ds(row + 288, 16), lanes] = even_tile(18) + odd_tile(0)
    for i in range(1, 19):
        grouped[pl.ds(row + 288 + 16 * i, 16), lanes] = odd_tile(i)


def group(labels, even, odd, grouped, p):
    wide = [jnp.broadcast_to(label, (16, 256)) for label in labels]

    def masks(kind):
        return [jnp.where(label == kind, 1.0, 0.0).astype(BF) for label in wide]

    first, second = masks(2 * p), masks(2 * p + 1)

    def total(ref, mask, i):
        terms = [ref[j, 16 * i : 16 * i + 16, :] * mask[j] for j in range(LIST)]
        while len(terms) > 1:
            terms = [terms[q] + terms[q + 1] for q in range(0, len(terms), 2)]
        return terms[0]

    stack_pair(
        grouped,
        pl.multiple_of(p * 2 * F, 16),
        slice(None),
        lambda i: total(even, first, i),
        lambda i: total(odd, second, i),
    )


def near_body(block, count, a_ref, b_ref, c_ref, src_ref, cls_ref, maps_ref, out_ref, window, even, odd, grouped):
    side = block % 2
    for k in range(4 + count):
        half = k + side
        window[:, 256 * k : 256 * k + 256] = (a_ref, b_ref, c_ref)[half // 2][:, 256 * (half % 2) : 256 * (half % 2) + 256]

    def pick(i, carry):
        local, four = i // 2, i % 2
        base = pl.multiple_of(local * 256, 256)
        lanes = pl.ds(pl.multiple_of((block + local) * 256, 256), 256)
        start = place() * 1024 - 512 + (block + local) * 256
        wanted = [onehot(src_ref[pl.ds(4 * four + q, 1), lanes] - start, 1280) for q in range(4)]
        value = dot(window[:, pl.ds(base, 1280)], jnp.concatenate(wanted, axis=1))
        for q in range(4):
            spread(value[:, 256 * q : 256 * q + 256], even.at[local], odd.at[local], 4 * four + q, slice(None))
        return carry

    lax.fori_loop(0, 2 * count, pick, 0)

    def sums(i, carry):
        local, p = i // 16, i % 16
        lanes = pl.ds(pl.multiple_of((block + local) * 256, 256), 256)
        labels = [cls_ref[j : j + 1, lanes] for j in range(LIST)]
        group(labels, even.at[local], odd.at[local], grouped.at[local], p)
        return carry

    lax.fori_loop(0, 16 * count, sums, 0)

    def send(i, carry):
        out_ref[i] = dot(maps_ref[...], grouped[i])
        return carry

    lax.fori_loop(0, count, send, 0)


def near(block, count, a, b, c, src, cls, maps):
    return pl.pallas_call(
        functools.partial(near_body, block, count),
        out_shape=jax.ShapeDtypeStruct((count, F, 256), F32),
        in_specs=[VM] * 6,
        out_specs=VM,
        scratch_shapes=[
            pltpu.VMEM((F, 1024 + 256 * count), BF),
            pltpu.VMEM((count, LIST, F + 8, 256), BF),
            pltpu.VMEM((count, LIST, F + 8, 256), BF),
            pltpu.VMEM((count, KINDS * F, 256), BF),
        ],
        compiler_params=pltpu.CompilerParams(vmem_limit_bytes=(22 if count > 1 else 16) * 2**20),
        cost_estimate=pl.CostEstimate(flops=count * 6 * 10**9, bytes_accessed=6 * 10**6, transcendentals=0),
        name=f"near{block}",
    )(a, b, c, src, cls, maps)


def turn_body(lower_ref, middle_ref, upper_ref, out_ref):
    parts = [ref[k].astype(F32) for ref in (lower_ref, middle_ref, upper_ref) for k in range(ref.shape[0])]
    out_ref[...] = jnp.concatenate(parts, axis=0).T.astype(BF)


def turn(lower, three, upper):
    return pl.pallas_call(
        turn_body,
        out_shape=jax.ShapeDtypeStruct((F, 128), BF),
        in_specs=[VM] * 3,
        out_specs=VM,
        compiler_params=pltpu.CompilerParams(vmem_limit_bytes=8 * 2**20),
        cost_estimate=pl.CostEstimate(flops=10**8, bytes_accessed=10**5, transcendentals=0),
        name="turn",
    )(lower, three, upper)


def halo_body(below_ref, above_ref, up_ref, out_ref, stack):
    children = jnp.concatenate([below_ref[...], above_ref[...]], axis=1)
    out_ref[...] = ascend(children, up_ref, stack).astype(BF)


def halo_six(below, above, up):
    return pl.pallas_call(
        halo_body,
        out_shape=jax.ShapeDtypeStruct((F, 128), BF),
        in_specs=[VM] * 3,
        out_specs=VM,
        scratch_shapes=[pltpu.VMEM((8 * F, 128), F32)],
        compiler_params=pltpu.CompilerParams(vmem_limit_bytes=16 * 2**20),
        cost_estimate=pl.CostEstimate(flops=2 * 10**9, bytes_accessed=3 * 10**6, transcendentals=0),
        name="halo",
    )(below, above, up)


def flip_body(down_ref, out_ref):
    out_ref[...] = down_ref[...].T


def flip(down):
    return pl.pallas_call(
        flip_body,
        out_shape=jax.ShapeDtypeStruct((8 * F, F), BF),
        in_specs=[VM],
        out_specs=VM,
        compiler_params=pltpu.CompilerParams(vmem_limit_bytes=16 * 2**20),
        cost_estimate=pl.CostEstimate(flops=10**9, bytes_accessed=3 * 10**6, transcendentals=0),
        name="flip",
    )(down)


def where_held(cell):
    cells, sub = lax.axis_index("cells"), lax.axis_index("sub")
    there = cell >> 6
    dz = ((there >> 3) - (cells >> 3) + 3) & 7
    dy = ((there >> 1) - (cells >> 1)) & 3
    dc = (there - cells) & 1
    dx = ((cell >> 4) - sub) & 3
    return (dc * 4 + dx) * 512 + dy * 128 + dz * 16 + (cell & 15)


def last_body(
    t0, t1, t2, t3, t4, t5, t6, t7, six_ref, halo_ref, src6_ref, cls6_ref, src5_ref, cls5_ref, src4_ref, cls4_ref,
    up_ref, down_ref,
    s0, s1, s2, maps_ref, out_ref,
    even, odd, grouped, stack, coarse, octants, weave, fars, local, src_ref, cls_ref,
):
    window = jnp.concatenate([six_ref[...], halo_ref[...]], axis=1)
    rel = src6_ref[...] - (place() * 128 - 64)
    src_ref[...] = jnp.where(rel < 64, rel + 128, jnp.where(rel < 192, rel - 64, rel))
    entry = lax.broadcasted_iota(jnp.int32, (8, 8), 0)
    column = lax.broadcasted_iota(jnp.int32, (8, 8), 1)
    four_labels = [
        jnp.sum(jnp.where(entry == column, cls4_ref[t : t + 1, :], 0).astype(F32), axis=1, keepdims=True)
        for t in range(2)
    ]
    unused = jnp.full((8, 110), KINDS, jnp.int32)
    cls_ref[:, :128] = jnp.concatenate([cls5_ref[...], *(x.astype(jnp.int32) for x in four_labels), unused], axis=1)
    cls_ref[:, 128:] = cls6_ref[...]

    def pick(i, carry):
        wanted = jnp.concatenate([src_ref[pl.ds(2 * i, 1), :], src_ref[pl.ds(2 * i + 1, 1), :]], axis=1)
        value = dot(window, onehot(wanted, 256))
        for q in range(2):
            spread(value[:, 128 * q : 128 * q + 128], even, odd, 2 * i + q, slice(128, 256))
        return carry

    lax.fori_loop(0, LIST // 2, pick, 0)

    entries_four = jnp.concatenate([src4_ref[0:1, :], src4_ref[1:2, :]], axis=1)
    wanted = jnp.concatenate(
        [src5_ref[j : j + 1, :] for j in range(LIST)] + [8 * entries_four + o for o in range(8)], axis=1
    )
    wanted = where_held(wanted)
    picked = jnp.zeros((F, 256), F32)
    for k, table in enumerate((t0, t1, t2, t3, t4, t5, t6, t7)):
        picked += dot(table[...], onehot(wanted - 512 * k, 512))
    stack[...] = jnp.zeros(stack.shape, F32)
    for o in range(8):
        stack[o * F : (o + 1) * F, :16] = picked[:, 128 + 16 * o : 144 + 16 * o]
    four = dot(up_ref[...], stack[...].astype(BF)).astype(BF).astype(F32)
    blank = jnp.zeros((F, 110), F32)
    for j in range(LIST):
        value = jnp.concatenate([picked[:, 16 * j : 16 * j + 16], four[:, j : j + 1], four[:, 8 + j : 9 + j], blank], axis=1)
        spread(value, even, odd, j, slice(0, 128))

    def sums(p, carry):
        group([cls_ref[j : j + 1, :] for j in range(LIST)], even, odd, grouped, p)
        return carry

    lax.fori_loop(0, KINDS // 2, sums, 0)
    coarse[...] = dot(maps_ref[...], grouped[...])

    def fill(o, carry):
        row = lax.broadcasted_iota(jnp.int32, (128, 1024), 0)
        cell = lax.broadcasted_iota(jnp.int32, (128, 1024), 1)
        weave[pl.ds(pl.multiple_of(o * 128, 128), 128), :] = jnp.where(cell == 8 * row + o, 1.0, 0.0).astype(BF)
        return carry

    lax.fori_loop(0, 8, fill, 0)
    lane = lax.broadcasted_iota(jnp.int32, (F, 128), 1)
    fars[0] = jnp.where(lane < 16, coarse[:, :128], 0.0)
    fars[1] = coarse[:, 128:]
    take = lax.broadcasted_iota(jnp.int32, (128, 128), 0) == lax.broadcasted_iota(jnp.int32, (128, 128), 1) + 16
    local[...] = dot(coarse[:, :128].astype(BF), jnp.where(take, 1.0, 0.0).astype(BF)).astype(BF)

    def woven(lanes):
        return dot(octants[...], weave[:, lanes])

    def fall(level, carry):
        children = dot(down_ref[...], local[...])
        for o in range(8):
            octants[:, 128 * o : 128 * o + 128] = children[o * F : (o + 1) * F, :].astype(BF)

        @pl.when(level < 2)
        def _():
            local[...] = (woven(slice(0, 128)) + fars[jnp.minimum(level, 1)]).astype(BF)

        return carry

    lax.fori_loop(0, 3, fall, 0)
    for q, seven in enumerate((s0.at[0], s1.at[0], s2.at[0], s2.at[1])):
        lanes = slice(256 * q, 256 * q + 256)
        out_ref[:, lanes] = (woven(lanes) + seven[...]).astype(BF)


def last(tables, six, halo, lists, up, down, sevens, maps):
    return pl.pallas_call(
        last_body,
        out_shape=jax.ShapeDtypeStruct((F, 1024), BF),
        in_specs=[VM] * 22,
        out_specs=VM,
        scratch_shapes=[
            pltpu.VMEM((LIST, F + 8, 256), BF),
            pltpu.VMEM((LIST, F + 8, 256), BF),
            pltpu.VMEM((KINDS * F, 256), BF),
            pltpu.VMEM((8 * F, 128), F32),
            pltpu.VMEM((F, 256), F32),
            pltpu.VMEM((F, 1024), BF),
            pltpu.VMEM((1024, 1024), BF),
            pltpu.VMEM((2, F, 128), F32),
            pltpu.VMEM((F, 128), BF),
            pltpu.VMEM((LIST, 128), jnp.int32),
            pltpu.VMEM((LIST, 256), jnp.int32),
        ],
        compiler_params=pltpu.CompilerParams(vmem_limit_bytes=24 * 2**20),
        cost_estimate=pl.CostEstimate(flops=8 * 10**9, bytes_accessed=12 * 10**6, transcendentals=0),
        name="last",
    )(*tables, six, halo, *lists, up, down, *sevens, maps)


def shifted(value, axis, steps):
    count = lax.axis_size(axis)
    first, last_one = (max(0, -steps), min(count, count - steps))
    return lax.ppermute(value, axis, [(source, source + steps) for source in range(first, last_one)])


def turned(value, axis, size, stride, steps):
    pairs = []
    for source in range(lax.axis_size(axis)):
        position = (source // stride) % size
        target = source + ((position + steps) % size - position) * stride
        pairs.append((source, target))
    return lax.ppermute(value, axis, pairs)


along_z = lambda value, steps: turned(value, "cells", 8, 8, steps)
along_y = lambda value, steps: turned(value, "cells", 4, 2, steps)
along_core = lambda value, steps: turned(value, "cells", 2, 1, steps)
along_x = lambda value, steps: turned(value, "sub", 4, 1, steps)


def tie(*values):
    return lax.optimization_barrier(values)


def body(
    leaf_multipoles,
    occupancy,
    upward_maps,
    transfer_maps,
    downward_maps,
    sources_seven,
    classes_seven,
    sources_six,
    classes_six,
    sources_five,
    classes_five,
    sources_four,
    classes_four,
):
    leaves = leaf_multipoles.T
    up, maps = upward_maps.T, transfer_maps.T
    masked = leaves * occupancy.astype(BF)[None, :]
    lo, hi = masked[:, :512], masked[:, 512:]
    below = shifted(hi, ("cells", "sub"), 1)
    above = shifted(lo, ("cells", "sub"), -1)
    six, five = rise(lo, hi, up)

    src_seven, cls_seven = sources_seven.T, classes_seven.T

    down = flip(downward_maps)
    minus, plus = along_z(five, 1), along_z(five, -1)
    three = jnp.stack([minus, five, plus])
    three, near_lo = tie(three, lo)
    upper = along_z(three, -3)
    lower = along_z(three[1:], 3)
    seven_0 = near(0, 1, below, near_lo, hi, src_seven, cls_seven, maps)
    lower, upper, seven_0 = tie(lower, upper, seven_0)
    column = turn(lower, three, upper)
    column, seven_0, near_lo = tie(column, seven_0, near_lo)
    sides = along_y(column, -1), along_y(column, 2), along_y(column, 1)
    seven_1 = near(1, 1, below, near_lo, hi, src_seven, cls_seven, maps)
    *sides, seven_1 = tie(*sides, seven_1)
    plane = jnp.concatenate([column, *sides], axis=1)
    plane, seven_1, near_lo = tie(plane, seven_1, near_lo)
    tables = [along_x(plane, -1), along_x(plane, 2), along_x(plane, 1)]
    other = along_core(plane, 1)
    seven_2 = near(2, 2, near_lo, hi, above, src_seven, cls_seven, maps)
    *tables, seven_2, late_up = tie(*tables, seven_2, up)
    tables = [plane, *tables, other] + [along_core(table, 1) for table in tables]
    halo = halo_six(below, above, late_up)
    sevens = [seven_0, seven_1, seven_2]

    lists = (
        sources_six.T,
        classes_six.T,
        sources_five.T,
        classes_five.T,
        sources_four,
        classes_four,
    )
    return last(tables, six, halo, lists, up, down, sevens, maps).T


def solution(mesh):
    in_specs = (
        P(("cells", "sub"), None),
        P(("cells", "sub")),
        P(),
        P(),
        P(),
        P(("cells", "sub"), None),
        P(("cells", "sub"), None),
        P(("cells", "sub"), None),
        P(("cells", "sub"), None),
        P(("cells", "sub"), None),
        P(("cells", "sub"), None),
        P(("cells", "sub"), None),
        P(("cells", "sub"), None),
    )
    out_specs = P(("cells", "sub"), None)
    return jax.shard_map(body, mesh=mesh, in_specs=in_specs, out_specs=out_specs, check_vma=False)
```

```python
import functools

import jax
import jax.numpy as jnp
from jax import lax
from jax.experimental import pallas as pl
from jax.experimental.pallas import tpu as pltpu
from jax.sharding import PartitionSpec as P

F = 296
KINDS = 32
LIST = 8
BF = jnp.bfloat16
F32 = jnp.float32
VM = pl.BlockSpec(memory_space=pltpu.VMEM)


def place():
    return lax.axis_index("cells") * 4 + lax.axis_index("sub")


def dot(a, b):
    return jnp.dot(a, b, preferred_element_type=F32)


def onehot(rel, depth):
    count = rel.shape[1]
    rows = lax.broadcasted_iota(jnp.int32, (depth, count), 0)
    return jnp.where(rows == rel, 1.0, 0.0).astype(BF)


def split_octants(children, first, width):
    count = children.shape[1]
    source = lax.broadcasted_iota(jnp.int32, (count, 2 * width), 0)
    place = lax.broadcasted_iota(jnp.int32, (count, 2 * width), 1)
    second = (place >= width).astype(jnp.int32)
    wanted = 8 * (place - width * second) + first + second
    return dot(children, jnp.where(source == wanted, 1.0, 0.0).astype(BF))


def ascend(children, up_ref, stack):
    count = children.shape[1]
    source = lax.broadcasted_iota(jnp.int32, (count, 1024), 0)
    column = lax.broadcasted_iota(jnp.int32, (1, 1024), 1)
    both = dot(children, jnp.where(source == 8 * (column & 127) + (column >> 7), 1.0, 0.0).astype(BF))
    for o in range(8):
        stack[o * F : (o + 1) * F, :] = both[:, 128 * o : 128 * o + 128]
    return dot(up_ref[...], stack[...].astype(BF))


def rise_body(lo_ref, hi_ref, up_ref, six_ref, five_ref, stack):
    children = jnp.concatenate([lo_ref[...], hi_ref[...]], axis=1)
    six = ascend(children, up_ref, stack).astype(BF)
    six_ref[...] = six
    source = lax.broadcasted_iota(jnp.int32, (128, 128), 0)
    column = lax.broadcasted_iota(jnp.int32, (1, 128), 1)
    both = dot(six, jnp.where(source == 8 * (column & 15) + (column >> 4), 1.0, 0.0).astype(BF))
    for o in range(8):
        stack[o * F : (o + 1) * F, :16] = both[:, 16 * o : 16 * o + 16]
    five = dot(up_ref[...], stack[...].astype(BF))
    five_ref[...] = five.T[:16, :].astype(BF)


def rise(lo, hi, up):
    return pl.pallas_call(
        rise_body,
        out_shape=(
            jax.ShapeDtypeStruct((F, 128), BF),
            jax.ShapeDtypeStruct((16, F), BF),
        ),
        in_specs=[VM] * 3,
        out_specs=(VM,) * 2,
        scratch_shapes=[pltpu.VMEM((8 * F, 128), F32)],
        compiler_params=pltpu.CompilerParams(vmem_limit_bytes=16 * 2**20),
        cost_estimate=pl.CostEstimate(flops=8 * 10**9, bytes_accessed=3 * 10**6, transcendentals=0),
        name="rise",
    )(lo, hi, up)


def spread(value, even, odd, slot, lanes):
    blank = jnp.zeros((8, value.shape[1]), F32)
    even[slot, :, lanes] = jnp.concatenate([value, blank], axis=0).astype(BF)
    odd[slot, :, lanes] = jnp.concatenate([blank, value], axis=0).astype(BF)


def stack_pair(grouped, row, lanes, even_tile, odd_tile):
    for i in range(18):
        grouped[pl.ds(row + 16 * i, 16), lanes] = even_tile(i)
    grouped[pl.ds(row + 288, 16), lanes] = even_tile(18) + odd_tile(0)
    for i in range(1, 19):
        grouped[pl.ds(row + 288 + 16 * i, 16), lanes] = odd_tile(i)


def group(labels, even, odd, grouped, p):
    wide = [jnp.broadcast_to(label, (16, 256)) for label in labels]

    def masks(kind):
        return [jnp.where(label == kind, 1.0, 0.0).astype(BF) for label in wide]

    first, second = masks(2 * p), masks(2 * p + 1)

    def total(ref, mask, i):
        terms = [ref[j, 16 * i : 16 * i + 16, :] * mask[j] for j in range(LIST)]
        while len(terms) > 1:
            terms = [terms[q] + terms[q + 1] for q in range(0, len(terms), 2)]
        return terms[0]

    stack_pair(
        grouped,
        pl.multiple_of(p * 2 * F, 16),
        slice(None),
        lambda i: total(even, first, i),
        lambda i: total(odd, second, i),
    )


def near_body(block, count, a_ref, b_ref, c_ref, src_ref, cls_ref, maps_ref, out_ref, window, even, odd, grouped):
    side = block % 2
    for k in range(4 + count):
        half = k + side
        window[:, 256 * k : 256 * k + 256] = (a_ref, b_ref, c_ref)[half // 2][:, 256 * (half % 2) : 256 * (half % 2) + 256]

    def pick(i, carry):
        local, four = i // 2, i % 2
        base = pl.multiple_of(local * 256, 256)
        lanes = pl.ds(pl.multiple_of((block + local) * 256, 256), 256)
        start = place() * 1024 - 512 + (block + local) * 256
        wanted = [onehot(src_ref[pl.ds(4 * four + q, 1), lanes] - start, 1280) for q in range(4)]
        value = dot(window[:, pl.ds(base, 1280)], jnp.concatenate(wanted, axis=1))
        for q in range(4):
            spread(value[:, 256 * q : 256 * q + 256], even.at[local], odd.at[local], 4 * four + q, slice(None))
        return carry

    lax.fori_loop(0, 2 * count, pick, 0)

    def sums(i, carry):
        local, p = i // 16, i % 16
        lanes = pl.ds(pl.multiple_of((block + local) * 256, 256), 256)
        labels = [cls_ref[j : j + 1, lanes] for j in range(LIST)]
        group(labels, even.at[local], odd.at[local], grouped.at[local], p)
        return carry

    lax.fori_loop(0, 16 * count, sums, 0)

    def send(i, carry):
        out_ref[i] = dot(maps_ref[...], grouped[i])
        return carry

    lax.fori_loop(0, count, send, 0)


def near(block, count, a, b, c, src, cls, maps):
    return pl.pallas_call(
        functools.partial(near_body, block, count),
        out_shape=jax.ShapeDtypeStruct((count, F, 256), F32),
        in_specs=[VM] * 6,
        out_specs=VM,
        scratch_shapes=[
            pltpu.VMEM((F, 1024 + 256 * count), BF),
            pltpu.VMEM((count, LIST, F + 8, 256), BF),
            pltpu.VMEM((count, LIST, F + 8, 256), BF),
            pltpu.VMEM((count, KINDS * F, 256), BF),
        ],
        compiler_params=pltpu.CompilerParams(vmem_limit_bytes=(22 if count > 1 else 16) * 2**20),
        cost_estimate=pl.CostEstimate(flops=count * 6 * 10**9, bytes_accessed=6 * 10**6, transcendentals=0),
        name=f"near{block}",
    )(a, b, c, src, cls, maps)


def turn_body(lower_ref, middle_ref, upper_ref, out_ref):
    parts = [ref[k].astype(F32) for ref in (lower_ref, middle_ref, upper_ref) for k in range(ref.shape[0])]
    out_ref[...] = jnp.concatenate(parts, axis=0).T.astype(BF)


def turn(lower, three, upper):
    return pl.pallas_call(
        turn_body,
        out_shape=jax.ShapeDtypeStruct((F, 128), BF),
        in_specs=[VM] * 3,
        out_specs=VM,
        compiler_params=pltpu.CompilerParams(vmem_limit_bytes=8 * 2**20),
        cost_estimate=pl.CostEstimate(flops=10**8, bytes_accessed=10**5, transcendentals=0),
        name="turn",
    )(lower, three, upper)


def halo_body(below_ref, above_ref, up_ref, out_ref, stack):
    children = jnp.concatenate([below_ref[...], above_ref[...]], axis=1)
    out_ref[...] = ascend(children, up_ref, stack).astype(BF)


def halo_six(below, above, up):
    return pl.pallas_call(
        halo_body,
        out_shape=jax.ShapeDtypeStruct((F, 128), BF),
        in_specs=[VM] * 3,
        out_specs=VM,
        scratch_shapes=[pltpu.VMEM((8 * F, 128), F32)],
        compiler_params=pltpu.CompilerParams(vmem_limit_bytes=16 * 2**20),
        cost_estimate=pl.CostEstimate(flops=2 * 10**9, bytes_accessed=3 * 10**6, transcendentals=0),
        name="halo",
    )(below, above, up)


def flip_body(down_ref, out_ref):
    out_ref[...] = down_ref[...].T


def flip(down):
    return pl.pallas_call(
        flip_body,
        out_shape=jax.ShapeDtypeStruct((8 * F, F), BF),
        in_specs=[VM],
        out_specs=VM,
        compiler_params=pltpu.CompilerParams(vmem_limit_bytes=16 * 2**20),
        cost_estimate=pl.CostEstimate(flops=10**9, bytes_accessed=3 * 10**6, transcendentals=0),
        name="flip",
    )(down)


def where_held(cell):
    cells, sub = lax.axis_index("cells"), lax.axis_index("sub")
    there = cell >> 6
    dz = ((there >> 3) - (cells >> 3) + 3) & 7
    dy = ((there >> 1) - (cells >> 1)) & 3
    dc = (there - cells) & 1
    dx = ((cell >> 4) - sub) & 3
    return (dc * 4 + dx) * 512 + dy * 128 + dz * 16 + (cell & 15)


def last_body(
    t0, t1, t2, t3, t4, t5, t6, t7, six_ref, halo_ref, src6_ref, cls6_ref, src5_ref, cls5_ref, src4_ref, cls4_ref,
    up_ref, down_ref,
    s0, s1, s2, maps_ref, out_ref,
    even, odd, grouped, stack, coarse, octants, weave, fars, local, src_ref, cls_ref,
):
    window = jnp.concatenate([six_ref[...], halo_ref[...]], axis=1)
    rel = src6_ref[...] - (place() * 128 - 64)
    src_ref[...] = jnp.where(rel < 64, rel + 128, jnp.where(rel < 192, rel - 64, rel))
    entry = lax.broadcasted_iota(jnp.int32, (8, 8), 0)
    column = lax.broadcasted_iota(jnp.int32, (8, 8), 1)
    four_labels = [
        jnp.sum(jnp.where(entry == column, cls4_ref[t : t + 1, :], 0).astype(F32), axis=1, keepdims=True)
        for t in range(2)
    ]
    unused = jnp.full((8, 110), KINDS, jnp.int32)
    cls_ref[:, :128] = jnp.concatenate([cls5_ref[...], *(x.astype(jnp.int32) for x in four_labels), unused], axis=1)
    cls_ref[:, 128:] = cls6_ref[...]

    def pick(i, carry):
        wanted = jnp.concatenate([src_ref[pl.ds(2 * i, 1), :], src_ref[pl.ds(2 * i + 1, 1), :]], axis=1)
        value = dot(window, onehot(wanted, 256))
        for q in range(2):
            spread(value[:, 128 * q : 128 * q + 128], even, odd, 2 * i + q, slice(128, 256))
        return carry

    lax.fori_loop(0, LIST // 2, pick, 0)

    entries_four = jnp.concatenate([src4_ref[0:1, :], src4_ref[1:2, :]], axis=1)
    wanted = jnp.concatenate(
        [src5_ref[j : j + 1, :] for j in range(LIST)] + [8 * entries_four + o for o in range(8)], axis=1
    )
    wanted = where_held(wanted)
    picked = jnp.zeros((F, 256), F32)
    for k, table in enumerate((t0, t1, t2, t3, t4, t5, t6, t7)):
        picked += dot(table[...], onehot(wanted - 512 * k, 512))
    stack[...] = jnp.zeros(stack.shape, F32)
    for o in range(8):
        stack[o * F : (o + 1) * F, :16] = picked[:, 128 + 16 * o : 144 + 16 * o]
    four = dot(up_ref[...], stack[...].astype(BF)).astype(BF).astype(F32)
    blank = jnp.zeros((F, 110), F32)
    for j in range(LIST):
        value = jnp.concatenate([picked[:, 16 * j : 16 * j + 16], four[:, j : j + 1], four[:, 8 + j : 9 + j], blank], axis=1)
        spread(value, even, odd, j, slice(0, 128))

    def sums(p, carry):
        group([cls_ref[j : j + 1, :] for j in range(LIST)], even, odd, grouped, p)
        return carry

    lax.fori_loop(0, KINDS // 2, sums, 0)
    coarse[...] = dot(maps_ref[...], grouped[...])

    def fill(o, carry):
        row = lax.broadcasted_iota(jnp.int32, (128, 1024), 0)
        cell = lax.broadcasted_iota(jnp.int32, (128, 1024), 1)
        weave[pl.ds(pl.multiple_of(o * 128, 128), 128), :] = jnp.where(cell == 8 * row + o, 1.0, 0.0).astype(BF)
        return carry

    lax.fori_loop(0, 8, fill, 0)
    lane = lax.broadcasted_iota(jnp.int32, (F, 128), 1)
    fars[0] = jnp.where(lane < 16, coarse[:, :128], 0.0)
    fars[1] = coarse[:, 128:]
    take = lax.broadcasted_iota(jnp.int32, (128, 128), 0) == lax.broadcasted_iota(jnp.int32, (128, 128), 1) + 16
    local[...] = dot(coarse[:, :128].astype(BF), jnp.where(take, 1.0, 0.0).astype(BF)).astype(BF)

    def woven(lanes):
        return dot(octants[...], weave[:, lanes])

    def fall(level, carry):
        children = dot(down_ref[...], local[...])
        for o in range(8):
            octants[:, 128 * o : 128 * o + 128] = children[o * F : (o + 1) * F, :].astype(BF)

        @pl.when(level < 2)
        def _():
            local[...] = (woven(slice(0, 128)) + fars[jnp.minimum(level, 1)]).astype(BF)

        return carry

    lax.fori_loop(0, 3, fall, 0)
    for q, seven in enumerate((s0.at[0], s1.at[0], s2.at[0], s2.at[1])):
        lanes = slice(256 * q, 256 * q + 256)
        out_ref[:, lanes] = (woven(lanes) + seven[...]).astype(BF)


def last(tables, six, halo, lists, up, down, sevens, maps):
    return pl.pallas_call(
        last_body,
        out_shape=jax.ShapeDtypeStruct((F, 1024), BF),
        in_specs=[VM] * 22,
        out_specs=VM,
        scratch_shapes=[
            pltpu.VMEM((LIST, F + 8, 256), BF),
            pltpu.VMEM((LIST, F + 8, 256), BF),
            pltpu.VMEM((KINDS * F, 256), BF),
            pltpu.VMEM((8 * F, 128), F32),
            pltpu.VMEM((F, 256), F32),
            pltpu.VMEM((F, 1024), BF),
            pltpu.VMEM((1024, 1024), BF),
            pltpu.VMEM((2, F, 128), F32),
            pltpu.VMEM((F, 128), BF),
            pltpu.VMEM((LIST, 128), jnp.int32),
            pltpu.VMEM((LIST, 256), jnp.int32),
        ],
        compiler_params=pltpu.CompilerParams(vmem_limit_bytes=24 * 2**20),
        cost_estimate=pl.CostEstimate(flops=8 * 10**9, bytes_accessed=12 * 10**6, transcendentals=0),
        name="last",
    )(*tables, six, halo, *lists, up, down, *sevens, maps)


def shifted(value, axis, steps):
    count = lax.axis_size(axis)
    first, last_one = (max(0, -steps), min(count, count - steps))
    return lax.ppermute(value, axis, [(source, source + steps) for source in range(first, last_one)])


def turned(value, axis, size, stride, steps):
    pairs = []
    for source in range(lax.axis_size(axis)):
        position = (source // stride) % size
        target = source + ((position + steps) % size - position) * stride
        pairs.append((source, target))
    return lax.ppermute(value, axis, pairs)


along_z = lambda value, steps: turned(value, "cells", 8, 8, steps)
along_y = lambda value, steps: turned(value, "cells", 4, 2, steps)
along_core = lambda value, steps: turned(value, "cells", 2, 1, steps)
along_x = lambda value, steps: turned(value, "sub", 4, 1, steps)


def tie(*values):
    return lax.optimization_barrier(values)


def body(
    leaf_multipoles,
    occupancy,
    upward_maps,
    transfer_maps,
    downward_maps,
    sources_seven,
    classes_seven,
    sources_six,
    classes_six,
    sources_five,
    classes_five,
    sources_four,
    classes_four,
):
    leaves = leaf_multipoles.T
    up, maps = upward_maps.T, transfer_maps.T
    rows = lax.broadcasted_iota(jnp.int32, leaves.shape, 0)
    masked = jnp.where(occupancy[None, :] + rows > rows, leaves, jnp.zeros_like(leaves))
    lo, hi = masked[:, :512], masked[:, 512:]
    below = shifted(hi, ("cells", "sub"), 1)
    above = shifted(lo, ("cells", "sub"), -1)
    six, five = rise(lo, hi, up)

    src_seven, cls_seven = sources_seven.T, classes_seven.T

    down = flip(downward_maps)
    minus, plus = along_z(five, 1), along_z(five, -1)
    three = jnp.stack([minus, five, plus])
    three, near_lo = tie(three, lo)
    upper = along_z(three, -3)
    lower = along_z(three[1:], 3)
    seven_0 = near(0, 1, below, near_lo, hi, src_seven, cls_seven, maps)
    lower, upper, seven_0 = tie(lower, upper, seven_0)
    column = turn(lower, three, upper)
    column, seven_0, near_lo = tie(column, seven_0, near_lo)
    sides = along_y(column, -1), along_y(column, 2), along_y(column, 1)
    seven_1 = near(1, 1, below, near_lo, hi, src_seven, cls_seven, maps)
    *sides, seven_1 = tie(*sides, seven_1)
    plane = jnp.concatenate([column, *sides], axis=1)
    plane, seven_1, near_lo = tie(plane, seven_1, near_lo)
    tables = [along_x(plane, -1), along_x(plane, 2), along_x(plane, 1)]
    other = along_core(plane, 1)
    seven_2 = near(2, 2, near_lo, hi, above, src_seven, cls_seven, maps)
    *tables, seven_2, late_up = tie(*tables, seven_2, up)
    tables = [plane, *tables, other] + [along_core(table, 1) for table in tables]
    halo = halo_six(below, above, late_up)
    sevens = [seven_0, seven_1, seven_2]

    lists = (
        sources_six.T,
        classes_six.T,
        sources_five.T,
        classes_five.T,
        sources_four,
        classes_four,
    )
    return last(tables, six, halo, lists, up, down, sevens, maps).T


def solution(mesh):
    in_specs = (
        P(("cells", "sub"), None),
        P(("cells", "sub")),
        P(),
        P(),
        P(),
        P(("cells", "sub"), None),
        P(("cells", "sub"), None),
        P(("cells", "sub"), None),
        P(("cells", "sub"), None),
        P(("cells", "sub"), None),
        P(("cells", "sub"), None),
        P(("cells", "sub"), None),
        P(("cells", "sub"), None),
    )
    out_specs = P(("cells", "sub"), None)
    return jax.shard_map(body, mesh=mesh, in_specs=in_specs, out_specs=out_specs, check_vma=False)
```
